32 devices in a mesh: row: 8 (over z, x), col: 4 (over y, core).
Axes of the slice: x: 2, y: 2, z: 4, core: 2. Of those that a mesh axis runs over, the one named last changes fastest.
Arguments:
- inverse_block: bfloat16 [10240, 10240], P('row', 'col'), may hold values from -6 to 6
- factor_cols: bfloat16 [10240, 1024], P('row', 'col'), may hold values from -0.078125 to 0.078125
- diag_inverse: float32 [4, 256, 256], P('col', 'row'), may hold values from -6 to 6
- fill_mask: int32 [40, 4], replicated, may hold values from 0 to 1
Outputs:
- inverse_cols: bfloat16 [10240, 1024], P('row', 'col')
- inverse_diag: float32 [4, 256, 256], P('col', 'row')
The draws below stay inside these ranges and needn't reach their ends.
All inputs are finite; a program needn't handle non-finite values.
Results may differ from the reference program's by a relative error of at most 0.0027.
Values may be sent and summed in bfloat16 or wider, within the bound.
A program may use at most 64 MiB of HBM per device.

```python
import jax
import jax.numpy as jnp
from jax import lax

W = 256
NBLK = 40
ORDER = 10240
SUPERNODES = 4
N_COL = 4


def draw_fill_mask(key, part):
    scores = jax.random.randint(key, (NBLK, SUPERNODES), 0, NBLK)
    levels = lax.broadcasted_iota(jnp.int32, (NBLK, SUPERNODES), 0)
    return (scores <= levels + NBLK // 4).astype(jnp.int32)


def block_scale(key, shape, pieces, least, high):
    level = 1.0
    for position, blocks in pieces:
        steps = jax.random.uniform(jax.random.fold_in(jax.random.fold_in(key, 6), position), (blocks,), jnp.float32, least / len(pieces), high / len(pieces))
        level = level * jnp.repeat(jnp.exp(steps), shape[position] // blocks).reshape((-1,) + (1,) * (len(shape) - 1 - position))
    return level


def noise(key, shape, scale, bound, pieces=(), held_as=jnp.bfloat16):
    values = scale * jax.random.normal(key, shape, jnp.float32)
    if pieces:
        values = values * block_scale(key, shape, pieces, -0.22, 0.18)
    return jnp.clip(values, -bound, bound).astype(held_as)


def setup_inputs(seed: int = 0) -> dict:
    key_of = jax.random.split(jax.random.key(seed), 5)
    return {
        "inverse_block": noise(key_of[0], (ORDER, ORDER), 1.0, 6.0, ((0, 8), (1, 4))),
        "factor_cols": noise(key_of[1], (ORDER, SUPERNODES * W), (ORDER // 2) ** -0.5, 0.078125, ((0, 8), (1, 4))),
        "diag_inverse": noise(key_of[2], (SUPERNODES, W, W), 1.0, 6.0, ((0, 4), (1, 8)), jnp.float32),
        "fill_mask": draw_fill_mask(jax.random.fold_in(key_of[4], 71), 0),
    }


def build_mask(fill_mask):
    block_count, node_count = fill_mask.shape
    expanded = jnp.broadcast_to(fill_mask[:, None, :], (block_count, W, node_count)).reshape(block_count * W, node_count)
    wide = jnp.broadcast_to(expanded[:, :, None], (block_count * W, node_count, W))
    return wide.reshape(block_count * W, node_count * W)


def reference(inverse_block, factor_cols, diag_inverse, fill_mask):
    column_mask = build_mask(fill_mask)
    selected = factor_cols * column_mask.astype(jnp.bfloat16)
    block_width = ORDER // N_COL

    def add_block(index, running):
        start = (index * block_width).astype(jnp.int32)
        inverse_piece = lax.dynamic_slice_in_dim(inverse_block, start, block_width, 1)
        factor_rows = lax.dynamic_slice_in_dim(selected, start, block_width, 0)
        product = jnp.dot(inverse_piece, factor_rows, preferred_element_type=jnp.float32)
        return running + product

    initial = jnp.zeros((ORDER, selected.shape[1]), jnp.float32)
    summed = lax.fori_loop(jnp.int32(0), jnp.int32(N_COL), add_block, initial)
    inverse_cols = (-summed * column_mask.astype(jnp.float32)).astype(jnp.bfloat16)
    node_count = fill_mask.shape[1]
    left_side = selected.astype(jnp.float32).reshape(ORDER, node_count, W)
    right_side = inverse_cols.astype(jnp.float32).reshape(ORDER, node_count, W)
    correction = jnp.einsum("isa,isb->sab", left_side, right_side)
    inverse_diag = diag_inverse - correction
    return inverse_cols, inverse_diag
```

```python
import functools
import math

import jax
import jax.numpy as jnp
from jax import lax
from jax.experimental import pallas as pl
from jax.experimental.pallas import tpu as pltpu
from jax.sharding import PartitionSpec as P

LANES = 128
PARTS = 4
TILES = 4
MESH = pl.DeviceIdType.MESH


def split_rows(extent, most):
    return max(n for n in range(1, most + 1) if extent % n == 0 and (extent // n) % 16 == 0)


def kernel(
    R, C, X, mask_ref, factor_ref, diag_ref, a_hbm, out_ref, diag_out_ref,
    a_ref, zbuf, fbuf, part, pair_recv, ysend, yrecv, corr, corr_recv,
    a_sem, z_send, z_recv, b_send, f_recv, x_send, x_recv,
    p_send, p_recv, y_send, y_recv, c_send, c_recv,
):
    Z, G, M = R // X, R // C, C // 2
    rows, cols = factor_ref.shape
    halves = cols // LANES
    width = diag_ref.shape[-1]
    diag_rows = diag_ref.shape[1]
    parts, tiles = z_recv.shape[1] // halves, p_send.shape[1]
    J = halves * parts
    pr, mt = rows // parts, rows // tiles
    r, c = lax.axis_index("row"), lax.axis_index("col")
    z, x = r // X, r % X
    m, k = c // 2, c % 2
    pending = []

    a_copy = pltpu.make_async_copy(a_hbm, a_ref, a_sem)
    a_copy.start()

    barrier = pltpu.get_barrier_semaphore()
    for step in range(1, R):
        pl.semaphore_signal(barrier, inc=1, device_id=((r + step) % R, c), device_id_type=MESH)
    for step in range(1, C):
        pl.semaphore_signal(barrier, inc=1, device_id=(r, (c + step) % C), device_id_type=MESH)

    unit = math.gcd(rows, width)

    def mask_of(index, half):
        block = (r * rows + index * unit) // width
        node = c * (cols // width) + (half * LANES) // width
        return mask_ref[block, node].astype(jnp.float32)

    for half in range(halves):
        for index in range(rows // unit):
            there = pl.ds(index * unit, unit)
            value = factor_ref[there, half * LANES:(half + 1) * LANES].astype(jnp.float32)
            zbuf[z, half, there, :] = (value * mask_of(index, half)).astype(jnp.bfloat16)

    pl.semaphore_wait(barrier, R - 1 + C - 1)

    def start(copy, condition=None):
        pending.append((copy, condition))
        if condition is None:
            copy.start()
        else:
            pl.when(condition)(copy.start)

    def place(j):
        return j // parts, pl.ds((j % parts) * pr, pr)

    def along_z(plane, j, up, condition):
        half, span = place(j)
        piece = zbuf.at[plane, half, span]
        start(pltpu.make_async_remote_copy(
            src_ref=piece, dst_ref=piece,
            send_sem=z_send.at[0 if up else 1, plane, j], recv_sem=z_recv.at[plane, j],
            device_id=(r + X if up else r - X, c), device_id_type=MESH), condition)

    def to_owner(plane, j, condition):
        half, span = place(j)
        source = plane * X + x
        owner, g = source // G, source % G
        at = pl.multiple_of(g * rows + (j % parts) * pr, 16)
        dst = fbuf.at[half, pl.ds(at, pr), pl.ds(pl.multiple_of(c * LANES, LANES), LANES)]
        piece = zbuf.at[plane, half, span]
        here, away = owner == c, owner != c
        if condition is not None:
            here, away = jnp.logical_and(condition, here), jnp.logical_and(condition, away)
        local = pltpu.make_async_copy(piece, dst, f_recv.at[g, c, j])
        pl.when(here)(local.start)
        start(pltpu.make_async_remote_copy(
            src_ref=piece, dst_ref=dst, send_sem=b_send.at[plane, j], recv_sem=f_recv.at[g, c, j],
            device_id=(r, owner), device_id_type=MESH), away)

    def own(j):
        along_z(z, j, True, z + 1 < Z)
        along_z(z, j, False, z > 0)
        to_owner(z, j, None)

    def arrivals(j, d):
        half, span = place(j)
        for up in (True, False):
            plane = z - d if up else z + d
            there = z >= d if up else z + d < Z
            safe = jnp.clip(plane, 0, Z - 1)
            piece = zbuf.at[safe, half, span]
            pl.when(there)(pltpu.make_async_copy(piece, piece, z_recv.at[safe, j]).wait)
            if d < Z - 1:
                onward = z + 1 < Z if up else z > 0
                along_z(safe, j, up, jnp.logical_and(there, onward))
            to_owner(safe, j, there)

    def slab(g, j):
        half, _ = place(j)
        return fbuf.at[half, pl.ds(g * rows + (j % parts) * pr, pr)]

    def forward(j):
        half, _ = place(j)
        for g in range(G):
            mine = (G * c + g) % X == x
            whole = slab(g, j)

            @pl.when(mine)
            def _():
                for other in range(C):
                    piece = fbuf.at[half, pl.ds(g * rows + (j % parts) * pr, pr), pl.ds(other * LANES, LANES)]
                    pltpu.make_async_copy(piece, piece, f_recv.at[g, other, j]).wait()

            for dx in range(1, X):
                start(pltpu.make_async_remote_copy(
                    src_ref=whole, dst_ref=whole, send_sem=x_send.at[dx - 1, g, j], recv_sem=x_recv.at[g, j],
                    device_id=(z * X + (x + dx) % X, c), device_id_type=MESH), mine)

    def gather_done(half):
        for p in range(parts):
            j = half * parts + p
            for g in range(G):
                whole = slab(g, j)
                pl.when((G * c + g) % X != x)(
                    pltpu.make_async_copy(whole, whole, x_recv.at[g, j]).wait)

    def multiply(half, t):
        span = pl.ds(t * mt, mt)
        value = jnp.dot(a_ref[span, :], fbuf[half], preferred_element_type=jnp.float32)
        for other in range(C):
            part[half, other % 2, other // 2, span, :] = value[:, other * LANES:(other + 1) * LANES]
        start(pltpu.make_async_remote_copy(
            src_ref=part.at[half, 1 - k, :, span], dst_ref=pair_recv.at[half, :, span],
            send_sem=p_send.at[half, t], recv_sem=p_recv.at[half, t],
            device_id=(r, m * 2 + 1 - k), device_id_type=MESH))

    def pair_sum(half, t):
        span = pl.ds(t * mt, mt)
        piece = pair_recv.at[half, :, span]
        pltpu.make_async_copy(piece, piece, p_recv.at[half, t]).wait()
        for dm in range(1, M):
            to = (m + dm) % M
            ysend[half, dm - 1, span, :] = part[half, k, to, span, :] + pair_recv[half, to, span, :]
            start(pltpu.make_async_remote_copy(
                src_ref=ysend.at[half, dm - 1, span], dst_ref=yrecv.at[half, dm - 1, span],
                send_sem=y_send.at[half, dm - 1, t], recv_sem=y_recv.at[half, dm - 1, t],
                device_id=(r, to * 2 + k), device_id_type=MESH))

    def finish(half, t):
        span = pl.ds(t * mt, mt)
        total = part[half, k, m, span, :] + pair_recv[half, m, span, :]
        for dm in range(1, M):
            piece = yrecv.at[half, dm - 1, span]
            pltpu.make_async_copy(piece, piece, y_recv.at[half, dm - 1, t]).wait()
            total = total + yrecv[half, dm - 1, span, :]
        part[half, k, m, span, :] = total

    def correct(half):
        lanes = slice(half * LANES, (half + 1) * LANES)
        for index in range(rows // unit):
            there = pl.ds(index * unit, unit)
            value = -part[half, k, m, there, :] * mask_of(index, half)
            out_ref[there, lanes] = value.astype(jnp.bfloat16)
        for left in range(halves):
            corr[half, left * LANES:(left + 1) * LANES, :] = lax.dot_general(
                zbuf[z, left], out_ref[:, lanes], (((0,), (0,)), ((), ())),
                preferred_element_type=jnp.float32)
        for step in range(1, R):
            to = (r + step) % R
            start(pltpu.make_async_remote_copy(
                src_ref=corr.at[half, pl.ds(pl.multiple_of(to * diag_rows, 8), diag_rows)],
                dst_ref=corr_recv.at[half, step - 1],
                send_sem=c_send.at[half, step - 1], recv_sem=c_recv.at[half, step - 1],
                device_id=(to, c), device_id_type=MESH))

    def diagonal(half):
        lanes = slice(half * LANES, (half + 1) * LANES)
        total = corr[half, pl.ds(pl.multiple_of(r * diag_rows, 8), diag_rows), :]
        for step in range(1, R):
            piece = corr_recv.at[half, step - 1]
            pltpu.make_async_copy(piece, piece, c_recv.at[half, step - 1]).wait()
            total = total + corr_recv[half, step - 1]
        diag_out_ref[0, :, lanes] = diag_ref[0, :, lanes] - total

    own(0)
    jobs = []
    for j in range(J):
        for d in range(1, Z):
            arrivals(j, d)
            if d == 1 and j + 1 < J:
                own(j + 1)
        if j >= 1:
            forward(j - 1)
        for job in jobs[:3]:
            job()
        jobs = jobs[3:]
        if j >= 1 and j % parts == 0:
            half = j // parts - 1

            def ready(half=half):
                if half == 0:
                    a_copy.wait()
                gather_done(half)

            jobs.append(ready)
            for t in range(tiles):
                jobs.append(functools.partial(multiply, half, t))
            for t in range(tiles):
                jobs.append(functools.partial(pair_sum, half, t))
    forward(J - 1)
    for job in jobs:
        job()
    last = halves - 1
    for half in range(last):
        for t in range(tiles):
            finish(half, t)
        correct(half)
    if last == 0:
        a_copy.wait()
    gather_done(last)
    for t in range(tiles):
        multiply(last, t)
        if t >= 1:
            pair_sum(last, t - 1)
    pair_sum(last, tiles - 1)
    for half in range(last):
        diagonal(half)
    for t in range(tiles):
        finish(last, t)
    correct(last)
    diagonal(last)
    for copy, condition in pending:
        if condition is None:
            copy.wait_send()
        else:
            pl.when(condition)(copy.wait_send)


def body(R, C, inverse_block, factor_cols, diag_inverse, fill_mask):
    rows, cols = factor_cols.shape
    depth = inverse_block.shape[1]
    diag_rows, width = diag_inverse.shape[1:]
    X = max(n for n in range(1, R + 1) if R % n == 0 and n * n <= R)
    Z, G, M = R // X, R // C, C // 2
    halves = cols // LANES
    parts, tiles = split_rows(rows, PARTS), split_rows(rows, TILES)
    J = halves * parts
    dma = pltpu.SemaphoreType.DMA
    vmem = pl.BlockSpec(memory_space=pltpu.VMEM)
    return pl.pallas_call(
        functools.partial(kernel, R, C, X),
        out_shape=(
            jax.ShapeDtypeStruct((rows, cols), jnp.bfloat16),
            jax.ShapeDtypeStruct(diag_inverse.shape, jnp.float32),
        ),
        in_specs=[pl.BlockSpec(memory_space=pltpu.SMEM), vmem, vmem, pl.BlockSpec(memory_space=pl.ANY)],
        out_specs=(vmem, vmem),
        scratch_shapes=[
            pltpu.VMEM(inverse_block.shape, jnp.bfloat16),
            pltpu.VMEM((Z, halves, rows, LANES), jnp.bfloat16),
            pltpu.VMEM((halves, depth, C * LANES), jnp.bfloat16),
            pltpu.VMEM((halves, 2, M, rows, LANES), jnp.float32),
            pltpu.VMEM((halves, M, rows, LANES), jnp.float32),
            pltpu.VMEM((halves, max(M - 1, 1), rows, LANES), jnp.float32),
            pltpu.VMEM((halves, max(M - 1, 1), rows, LANES), jnp.float32),
            pltpu.VMEM((halves, width, LANES), jnp.float32),
            pltpu.VMEM((halves, R - 1, diag_rows, LANES), jnp.float32),
            dma(()),
            dma((2, Z, J)), dma((Z, J)), dma((Z, J)), dma((G, C, J)),
            dma((max(X - 1, 1), G, J)), dma((G, J)),
            dma((halves, tiles)), dma((halves, tiles)),
            dma((halves, max(M - 1, 1), tiles)), dma((halves, max(M - 1, 1), tiles)),
            dma((halves, R - 1)), dma((halves, R - 1)),
        ],
        compiler_params=pltpu.CompilerParams(
            collective_id=0, has_side_effects=True, vmem_limit_bytes=60 << 20
        ),
        cost_estimate=pl.CostEstimate(
            flops=2 * rows * depth * cols * C, bytes_accessed=2 * rows * depth, transcendentals=0
        ),
    )(fill_mask, factor_cols, diag_inverse, inverse_block)


def solution(mesh):
    placed = (P("row", "col"), P("row", "col"), P("col", "row", None), P())
    return jax.shard_map(
        functools.partial(body, mesh.shape["row"], mesh.shape["col"]),
        mesh=mesh,
        in_specs=placed,
        out_specs=(P("row", "col"), P("col", "row", None)),
        check_vma=False,
    )
```

```python
import functools
import math

import jax
import jax.numpy as jnp
from jax import lax
from jax.experimental import pallas as pl
from jax.experimental.pallas import tpu as pltpu
from jax.sharding import PartitionSpec as P

LANES = 128
PARTS = 2
TILES = 4
DELAY = 1
MESH = pl.DeviceIdType.MESH


def split_rows(extent, most):
    return max(n for n in range(1, most + 1) if extent % n == 0 and (extent // n) % 16 == 0)


def kernel(
    R, C, X, mask_ref, factor_ref, diag_ref, a_hbm, out_ref, diag_out_ref,
    a_ref, own_ref, zbuf, fbuf, part, pair_recv, ysend, yrecv, corr, corr_recv,
    a_sem, swap_send, swap_recv, z_send, z_recv, b_send, f_recv, x_send, x_recv,
    p_send, p_recv, y_send, y_recv, c_send, c_recv,
):
    Z, G, M = R // X, R // C, C // 2
    rows, cols = factor_ref.shape
    halves = cols // LANES
    quarters = [(kk, half) for half in range(halves) for kk in range(2)]
    Q = len(quarters)
    width = diag_ref.shape[-1]
    diag_rows = diag_ref.shape[1]
    J, tiles = z_recv.shape[1], p_send.shape[1]
    parts = J // Q
    depth = rows // 2
    pr, mt = depth // parts, rows // tiles
    r, c = lax.axis_index("row"), lax.axis_index("col")
    z, x = r // X, r % X
    m, k = c // 2, c % 2
    partner = m * 2 + 1 - k
    pending = []

    a_copy = pltpu.make_async_copy(a_hbm, a_ref, a_sem)
    a_copy.start()

    barrier = pltpu.get_barrier_semaphore()
    for step in range(1, R):
        pl.semaphore_signal(barrier, inc=1, device_id=((r + step) % R, c), device_id_type=MESH)
    for step in range(1, C):
        pl.semaphore_signal(barrier, inc=1, device_id=(r, (c + step) % C), device_id_type=MESH)

    unit = math.gcd(rows, width)

    def mask_of(index, half):
        block = (r * rows + index * unit) // width
        node = c * (cols // width) + (half * LANES) // width
        return mask_ref[node, block].astype(jnp.float32)

    for half in range(halves):
        for index in range(rows // unit):
            there = pl.ds(index * unit, unit)
            value = factor_ref[there, half * LANES:(half + 1) * LANES].astype(jnp.float32)
            own_ref[half, there, :] = (value * mask_of(index, half)).astype(jnp.bfloat16)

    pl.semaphore_wait(barrier, R - 1 + C - 1)

    def start(copy, condition=None):
        pending.append((copy, condition))
        if condition is None:
            copy.start()
        else:
            pl.when(condition)(copy.start)

    def half_rows(index):
        return pl.ds(pl.multiple_of(index * depth, 16), depth)

    for half in range(halves):
        start(pltpu.make_async_remote_copy(
            src_ref=own_ref.at[half, half_rows(1 - k)], dst_ref=zbuf.at[z, half * 2 + k],
            send_sem=swap_send.at[half], recv_sem=swap_recv.at[half],
            device_id=(r, partner), device_id_type=MESH))
    for half in range(halves):
        zbuf[z, half * 2 + k] = own_ref[half, half_rows(k), :]

    def place(j):
        return j // parts, pl.ds((j % parts) * pr, pr)

    def along_z(plane, j, up, condition):
        q, span = place(j)
        piece = zbuf.at[plane, q, span]
        start(pltpu.make_async_remote_copy(
            src_ref=piece, dst_ref=piece,
            send_sem=z_send.at[0 if up else 1, plane, j], recv_sem=z_recv.at[plane, j],
            device_id=(r + X if up else r - X, c), device_id_type=MESH), condition)

    def to_owner(plane, j, condition):
        q, span = place(j)
        source = plane * X + x
        owner, g = source // G, source % G
        dst = fbuf.at[q, g, k, span, pl.ds(pl.multiple_of(m * LANES, LANES), LANES)]
        piece = zbuf.at[plane, q, span]
        here, away = owner == c, owner != c
        if condition is not None:
            here, away = jnp.logical_and(condition, here), jnp.logical_and(condition, away)
        local = pltpu.make_async_copy(piece, dst, f_recv.at[g, c, j])
        pl.when(here)(local.start)
        start(pltpu.make_async_remote_copy(
            src_ref=piece, dst_ref=dst, send_sem=b_send.at[plane, j], recv_sem=f_recv.at[g, c, j],
            device_id=(r, owner), device_id_type=MESH), away)

    def own(j):
        q = j // parts
        kk, half = quarters[q]
        if j % parts == 0:
            piece = zbuf.at[z, q]
            pl.when(k != kk)(pltpu.make_async_copy(piece, piece, swap_recv.at[half]).wait)
        along_z(z, j, True, z + 1 < Z)
        along_z(z, j, False, z > 0)
        to_owner(z, j, None)

    def arrivals(j, d):
        q, span = place(j)
        for up in (True, False):
            plane = z - d if up else z + d
            there = z >= d if up else z + d < Z
            safe = jnp.clip(plane, 0, Z - 1)
            piece = zbuf.at[safe, q, span]
            pl.when(there)(pltpu.make_async_copy(piece, piece, z_recv.at[safe, j]).wait)
            if d < Z - 1:
                onward = z + 1 < Z if up else z > 0
                along_z(safe, j, up, jnp.logical_and(there, onward))
            to_owner(safe, j, there)

    def forward(j):
        q, span = place(j)
        for g in range(G):
            mine = (G * c + g) % X == x
            whole = fbuf.at[q, g, :, span]

            @pl.when(mine)
            def _():
                for other in range(C):
                    piece = fbuf.at[q, g, other % 2, span, pl.ds(other // 2 * LANES, LANES)]
                    pltpu.make_async_copy(piece, piece, f_recv.at[g, other, j]).wait()

            for dx in range(1, X):
                start(pltpu.make_async_remote_copy(
                    src_ref=whole, dst_ref=whole, send_sem=x_send.at[dx - 1, g, j], recv_sem=x_recv.at[g, j],
                    device_id=(z * X + (x + dx) % X, c), device_id_type=MESH), mine)

    def gather_done(q):
        if q == 0:
            a_copy.wait()
        for p in range(parts):
            j = q * parts + p
            _, span = place(j)
            for g in range(G):
                whole = fbuf.at[q, g, :, span]
                pl.when((G * c + g) % X != x)(
                    pltpu.make_async_copy(whole, whole, x_recv.at[g, j]).wait)

    def multiply(q, t):
        kk, _ = quarters[q]
        span = pl.ds(t * mt, mt)
        panel = fbuf[q].reshape(G * rows, M * LANES)
        value = jnp.dot(a_ref[span, :], panel, preferred_element_type=jnp.float32)
        for to in range(M):
            part[q, to, span, :] = value[:, to * LANES:(to + 1) * LANES]
        start(pltpu.make_async_remote_copy(
            src_ref=part.at[q, :, span], dst_ref=pair_recv.at[q, :, span],
            send_sem=p_send.at[q, t], recv_sem=p_recv.at[q, t],
            device_id=(r, partner), device_id_type=MESH), k != kk)

    def pair_sum(q, t):
        kk, half = quarters[q]
        span = pl.ds(t * mt, mt)
        piece = pair_recv.at[q, :, span]

        @pl.when(k == kk)
        def _():
            pltpu.make_async_copy(piece, piece, p_recv.at[q, t]).wait()
            for dm in range(1, M):
                to = (m + dm) % M
                ysend[half, dm - 1, span, :] = part[q, to, span, :] + pair_recv[q, to, span, :]

        for dm in range(1, M):
            to = (m + dm) % M
            start(pltpu.make_async_remote_copy(
                src_ref=ysend.at[half, dm - 1, span], dst_ref=yrecv.at[half, dm - 1, span],
                send_sem=y_send.at[q, dm - 1, t], recv_sem=y_recv.at[q, dm - 1, t],
                device_id=(r, to * 2 + k), device_id_type=MESH), k == kk)

    def finish(q):
        kk, half = quarters[q]
        lanes = slice(half * LANES, (half + 1) * LANES)

        @pl.when(k == kk)
        def _():
            for t in range(tiles):
                span = pl.ds(t * mt, mt)
                total = part[q, m, span, :] + pair_recv[q, m, span, :]
                for dm in range(1, M):
                    piece = yrecv.at[half, dm - 1, span]
                    pltpu.make_async_copy(piece, piece, y_recv.at[q, dm - 1, t]).wait()
                    total = total + yrecv[half, dm - 1, span, :]
                part[q, m, span, :] = total
            for index in range(rows // unit):
                there = pl.ds(index * unit, unit)
                value = -part[q, m, there, :] * mask_of(index, half)
                out_ref[there, lanes] = value.astype(jnp.bfloat16)
            for left in range(halves):
                corr[half, left * LANES:(left + 1) * LANES, :] = lax.dot_general(
                    own_ref[left], out_ref[:, lanes], (((0,), (0,)), ((), ())),
                    preferred_element_type=jnp.float32)

        for step in range(1, R):
            to = (r + step) % R
            start(pltpu.make_async_remote_copy(
                src_ref=corr.at[half, pl.ds(pl.multiple_of(to * diag_rows, 8), diag_rows)],
                dst_ref=corr_recv.at[half, step - 1],
                send_sem=c_send.at[half, step - 1], recv_sem=c_recv.at[half, step - 1],
                device_id=(to, c), device_id_type=MESH), k == kk)

    def diagonal(q):
        kk, half = quarters[q]
        lanes = slice(half * LANES, (half + 1) * LANES)

        @pl.when(k == kk)
        def _():
            total = corr[half, pl.ds(pl.multiple_of(r * diag_rows, 8), diag_rows), :]
            for step in range(1, R):
                piece = corr_recv.at[half, step - 1]
                pltpu.make_async_copy(piece, piece, c_recv.at[half, step - 1]).wait()
                total = total + corr_recv[half, step - 1]
            diag_out_ref[0, :, lanes] = diag_ref[0, :, lanes] - total

    def work(q):
        def first():
            gather_done(q)
            multiply(q, 0)

        def sums():
            for t in range(tiles):
                pair_sum(q, t)

        jobs = [first] + [functools.partial(multiply, q, t) for t in range(1, tiles)] + [sums]
        if q >= 1:
            jobs.append(functools.partial(finish, q - 1))
        return jobs

    own(0)
    jobs, done = [], 0
    for j in range(J):
        for d in range(1, Z):
            arrivals(j, d)
            if d == 1 and j + 1 < J:
                own(j + 1)
            if jobs:
                jobs.pop(0)()
        if j >= 1:
            forward(j - 1)
        if j - DELAY >= (done + 1) * parts:
            jobs += work(done)
            done += 1
    forward(J - 1)
    for job in jobs:
        job()
    for q in range(done, Q):
        gather_done(q)
        for t in range(tiles):
            multiply(q, t)
            if t >= 1:
                pair_sum(q, t - 1)
        pair_sum(q, tiles - 1)
        if q >= 1:
            finish(q - 1)
    for q in range(Q - 1):
        diagonal(q)
    finish(Q - 1)
    diagonal(Q - 1)
    for copy, condition in pending:
        if condition is None:
            copy.wait_send()
        else:
            pl.when(condition)(copy.wait_send)


def body(R, C, inverse_block, factor_cols, diag_inverse, fill_mask):
    rows, cols = factor_cols.shape
    depth = inverse_block.shape[1]
    diag_rows, width = diag_inverse.shape[1:]
    X = max(n for n in range(1, R + 1) if R % n == 0 and n * n <= R)
    Z, G, M = R // X, R // C, C // 2
    halves = cols // LANES
    parts, tiles = split_rows(rows // 2, PARTS), split_rows(rows, TILES)
    Q = 2 * halves
    J = Q * parts
    dma = pltpu.SemaphoreType.DMA
    vmem = pl.BlockSpec(memory_space=pltpu.VMEM)
    return pl.pallas_call(
        functools.partial(kernel, R, C, X),
        out_shape=(
            jax.ShapeDtypeStruct((rows, cols), jnp.bfloat16),
            jax.ShapeDtypeStruct(diag_inverse.shape, jnp.float32),
        ),
        in_specs=[pl.BlockSpec(memory_space=pltpu.SMEM), vmem, vmem, pl.BlockSpec(memory_space=pl.ANY)],
        out_specs=(vmem, vmem),
        scratch_shapes=[
            pltpu.VMEM(inverse_block.shape, jnp.bfloat16),
            pltpu.VMEM((halves, rows, LANES), jnp.bfloat16),
            pltpu.VMEM((Z, Q, rows // 2, LANES), jnp.bfloat16),
            pltpu.VMEM((Q, G, 2, rows // 2, M * LANES), jnp.bfloat16),
            pltpu.VMEM((Q, M, rows, LANES), jnp.float32),
            pltpu.VMEM((Q, M, rows, LANES), jnp.float32),
            pltpu.VMEM((halves, max(M - 1, 1), rows, LANES), jnp.float32),
            pltpu.VMEM((halves, max(M - 1, 1), rows, LANES), jnp.float32),
            pltpu.VMEM((halves, width, LANES), jnp.float32),
            pltpu.VMEM((halves, R - 1, diag_rows, LANES), jnp.float32),
            dma(()), dma((halves,)), dma((halves,)),
            dma((2, Z, J)), dma((Z, J)), dma((Z, J)), dma((G, C, J)),
            dma((max(X - 1, 1), G, J)), dma((G, J)),
            dma((Q, tiles)), dma((Q, tiles)),
            dma((Q, max(M - 1, 1), tiles)), dma((Q, max(M - 1, 1), tiles)),
            dma((halves, R - 1)), dma((halves, R - 1)),
        ],
        compiler_params=pltpu.CompilerParams(
            collective_id=0, has_side_effects=True, vmem_limit_bytes=60 << 20
        ),
        cost_estimate=pl.CostEstimate(
            flops=2 * rows * depth * cols * C, bytes_accessed=2 * rows * depth, transcendentals=0
        ),
    )(fill_mask.T, factor_cols, diag_inverse, inverse_block)


def solution(mesh):
    placed = (P("row", "col"), P("row", "col"), P("col", "row", None), P())
    return jax.shard_map(
        functools.partial(body, mesh.shape["row"], mesh.shape["col"]),
        mesh=mesh,
        in_specs=placed,
        out_specs=(P("row", "col"), P("col", "row", None)),
        check_vma=False,
    )
```

```python
import functools
import math

import jax
import jax.numpy as jnp
from jax import lax
from jax.experimental import pallas as pl
from jax.experimental.pallas import tpu as pltpu
from jax.sharding import PartitionSpec as P

LANES = 128
PARTS = 2
TILES = 4
DELAY = 1
HOPS = 2
AHEAD = 2
MESH = pl.DeviceIdType.MESH


def split_rows(extent, most):
    return max(n for n in range(1, most + 1) if extent % n == 0 and (extent // n) % 16 == 0)


def kernel(
    R, C, X, mask_ref, factor_ref, diag_ref, a_hbm, out_ref, diag_out_ref,
    a_ref, own_ref, zbuf, fbuf, part, pair_recv, ysend, yrecv, corr, corr_recv,
    a_sem, swap_send, swap_recv, z_send, z_recv, b_send, f_recv, x_send, x_recv,
    p_send, p_recv, y_send, y_recv, c_send, c_recv,
):
    Z, G, M = R // X, R // C, C // 2
    rows, cols = factor_ref.shape
    halves = cols // LANES
    quarters = [(kk, half) for half in range(halves) for kk in range(2)]
    Q = len(quarters)
    width = diag_ref.shape[-1]
    diag_rows = diag_ref.shape[1]
    J, tiles = z_recv.shape[1], p_send.shape[1]
    parts = J // Q
    depth = rows // 2
    pr, mt = depth // parts, rows // tiles
    r, c = lax.axis_index("row"), lax.axis_index("col")
    z, x = r // X, r % X
    m, k = c // 2, c % 2
    partner = m * 2 + 1 - k
    pending = []

    a_copy = pltpu.make_async_copy(a_hbm, a_ref, a_sem)
    a_copy.start()

    barrier = pltpu.get_barrier_semaphore()
    for step in range(1, R):
        pl.semaphore_signal(barrier, inc=1, device_id=((r + step) % R, c), device_id_type=MESH)
    for step in range(1, C):
        pl.semaphore_signal(barrier, inc=1, device_id=(r, (c + step) % C), device_id_type=MESH)

    unit = math.gcd(rows, width)

    def mask_of(index, half):
        block = (r * rows + index * unit) // width
        node = c * (cols // width) + (half * LANES) // width
        return mask_ref[node, block].astype(jnp.float32)

    for half in range(halves):
        for index in range(rows // unit):
            there = pl.ds(index * unit, unit)
            value = factor_ref[there, half * LANES:(half + 1) * LANES].astype(jnp.float32)
            own_ref[half, there, :] = (value * mask_of(index, half)).astype(jnp.bfloat16)

    pl.semaphore_wait(barrier, R - 1 + C - 1)

    def start(copy, condition=None):
        pending.append((copy, condition))
        if condition is None:
            copy.start()
        else:
            pl.when(condition)(copy.start)

    def half_rows(index):
        return pl.ds(pl.multiple_of(index * depth, 16), depth)

    for half in range(halves):
        start(pltpu.make_async_remote_copy(
            src_ref=own_ref.at[half, half_rows(1 - k)], dst_ref=zbuf.at[z, half * 2 + k],
            send_sem=swap_send.at[half], recv_sem=swap_recv.at[half],
            device_id=(r, partner), device_id_type=MESH))
    for half in range(halves):
        zbuf[z, half * 2 + k] = own_ref[half, half_rows(k), :]

    def place(j):
        return j // parts, pl.ds((j % parts) * pr, pr)

    def along_z(plane, j, up, hops, condition):
        q, span = place(j)
        piece = zbuf.at[plane, q, span]
        start(pltpu.make_async_remote_copy(
            src_ref=piece, dst_ref=piece,
            send_sem=z_send.at[hops - 1, 0 if up else 1, plane, j], recv_sem=z_recv.at[plane, j],
            device_id=(r + X * hops if up else r - X * hops, c), device_id_type=MESH), condition)

    def to_owner(plane, j, condition):
        q, span = place(j)
        source = plane * X + x
        owner, g = source // G, source % G
        dst = fbuf.at[q, g, k, span, pl.ds(pl.multiple_of(m * LANES, LANES), LANES)]
        piece = zbuf.at[plane, q, span]
        here, away = owner == c, owner != c
        if condition is not None:
            here, away = jnp.logical_and(condition, here), jnp.logical_and(condition, away)
        local = pltpu.make_async_copy(piece, dst, f_recv.at[g, c, j])
        pl.when(here)(local.start)
        start(pltpu.make_async_remote_copy(
            src_ref=piece, dst_ref=dst, send_sem=b_send.at[plane, j], recv_sem=f_recv.at[g, c, j],
            device_id=(r, owner), device_id_type=MESH), away)

    def own(j):
        q = j // parts
        kk, half = quarters[q]
        if j % parts == 0:
            piece = zbuf.at[z, q]
            pl.when(k != kk)(pltpu.make_async_copy(piece, piece, swap_recv.at[half]).wait)
        for hops in range(1, HOPS + 1):
            along_z(z, j, True, hops, z + hops < Z)
            along_z(z, j, False, hops, z >= hops)
        to_owner(z, j, None)

    def arrivals(j, d):
        q, span = place(j)
        for up in (True, False):
            plane = z - d if up else z + d
            there = z >= d if up else z + d < Z
            safe = jnp.clip(plane, 0, Z - 1)
            piece = zbuf.at[safe, q, span]
            pl.when(there)(pltpu.make_async_copy(piece, piece, z_recv.at[safe, j]).wait)
            if HOPS <= d < Z - 1:
                onward = z + 1 < Z if up else z > 0
                along_z(safe, j, up, 1, jnp.logical_and(there, onward))
            to_owner(safe, j, there)

    def forward(j):
        q, span = place(j)
        for g in range(G):
            mine = (G * c + g) % X == x
            whole = fbuf.at[q, g, :, span]

            @pl.when(mine)
            def _():
                for other in range(C):
                    piece = fbuf.at[q, g, other % 2, span, pl.ds(other // 2 * LANES, LANES)]
                    pltpu.make_async_copy(piece, piece, f_recv.at[g, other, j]).wait()

            for dx in range(1, X):
                start(pltpu.make_async_remote_copy(
                    src_ref=whole, dst_ref=whole, send_sem=x_send.at[dx - 1, g, j], recv_sem=x_recv.at[g, j],
                    device_id=(z * X + (x + dx) % X, c), device_id_type=MESH), mine)

    def gather_done(q):
        if q == 0:
            a_copy.wait()
        for p in range(parts):
            j = q * parts + p
            _, span = place(j)
            for g in range(G):
                whole = fbuf.at[q, g, :, span]
                pl.when((G * c + g) % X != x)(
                    pltpu.make_async_copy(whole, whole, x_recv.at[g, j]).wait)

    def multiply(q, t):
        kk, _ = quarters[q]
        span = pl.ds(t * mt, mt)
        panel = fbuf[q].reshape(G * rows, M * LANES)
        value = jnp.dot(a_ref[span, :], panel, preferred_element_type=jnp.float32)
        for to in range(M):
            part[q, to, span, :] = value[:, to * LANES:(to + 1) * LANES]
        start(pltpu.make_async_remote_copy(
            src_ref=part.at[q, :, span], dst_ref=pair_recv.at[q, :, span],
            send_sem=p_send.at[q, t], recv_sem=p_recv.at[q, t],
            device_id=(r, partner), device_id_type=MESH), k != kk)

    def pair_sum(q, t):
        kk, half = quarters[q]
        span = pl.ds(t * mt, mt)
        piece = pair_recv.at[q, :, span]

        @pl.when(k == kk)
        def _():
            pltpu.make_async_copy(piece, piece, p_recv.at[q, t]).wait()
            for dm in range(1, M):
                to = (m + dm) % M
                ysend[half, dm - 1, span, :] = part[q, to, span, :] + pair_recv[q, to, span, :]

        for dm in range(1, M):
            to = (m + dm) % M
            start(pltpu.make_async_remote_copy(
                src_ref=ysend.at[half, dm - 1, span], dst_ref=yrecv.at[half, dm - 1, span],
                send_sem=y_send.at[q, dm - 1, t], recv_sem=y_recv.at[q, dm - 1, t],
                device_id=(r, to * 2 + k), device_id_type=MESH), k == kk)

    def finish(q):
        kk, half = quarters[q]
        lanes = slice(half * LANES, (half + 1) * LANES)

        @pl.when(k == kk)
        def _():
            for t in range(tiles):
                span = pl.ds(t * mt, mt)
                total = part[q, m, span, :] + pair_recv[q, m, span, :]
                for dm in range(1, M):
                    piece = yrecv.at[half, dm - 1, span]
                    pltpu.make_async_copy(piece, piece, y_recv.at[q, dm - 1, t]).wait()
                    total = total + yrecv[half, dm - 1, span, :]
                part[q, m, span, :] = total
            for index in range(rows // unit):
                there = pl.ds(index * unit, unit)
                value = -part[q, m, there, :] * mask_of(index, half)
                out_ref[there, lanes] = value.astype(jnp.bfloat16)
            for left in range(halves):
                corr[half, left * LANES:(left + 1) * LANES, :] = lax.dot_general(
                    own_ref[left], out_ref[:, lanes], (((0,), (0,)), ((), ())),
                    preferred_element_type=jnp.float32)

        for step in range(1, R):
            to = (r + step) % R
            start(pltpu.make_async_remote_copy(
                src_ref=corr.at[half, pl.ds(pl.multiple_of(to * diag_rows, 8), diag_rows)],
                dst_ref=corr_recv.at[half, step - 1],
                send_sem=c_send.at[half, step - 1], recv_sem=c_recv.at[half, step - 1],
                device_id=(to, c), device_id_type=MESH), k == kk)

    def diagonal(q):
        kk, half = quarters[q]
        lanes = slice(half * LANES, (half + 1) * LANES)

        @pl.when(k == kk)
        def _():
            total = corr[half, pl.ds(pl.multiple_of(r * diag_rows, 8), diag_rows), :]
            for step in range(1, R):
                piece = corr_recv.at[half, step - 1]
                pltpu.make_async_copy(piece, piece, c_recv.at[half, step - 1]).wait()
                total = total + corr_recv[half, step - 1]
            diag_out_ref[0, :, lanes] = diag_ref[0, :, lanes] - total

    def work(q):
        def first():
            gather_done(q)
            multiply(q, 0)

        def sums():
            for t in range(tiles):
                pair_sum(q, t)

        jobs = [first] + [functools.partial(multiply, q, t) for t in range(1, tiles)] + [sums]
        if q >= 1:
            jobs.append(functools.partial(finish, q - 1))
        return jobs

    for j in range(min(AHEAD, J)):
        own(j)
    jobs, done = [], 0
    for j in range(J):
        for d in range(1, Z):
            arrivals(j, d)
            if d == 1 and j + AHEAD < J:
                own(j + AHEAD)
            if jobs:
                jobs.pop(0)()
        if j >= 1:
            forward(j - 1)
        if j - DELAY >= (done + 1) * parts:
            jobs += work(done)
            done += 1
    forward(J - 1)
    for job in jobs:
        job()
    for q in range(done, Q):
        gather_done(q)
        for t in range(tiles):
            multiply(q, t)
            if t >= 1:
                pair_sum(q, t - 1)
        pair_sum(q, tiles - 1)
        if q >= 1:
            finish(q - 1)
    for q in range(Q - 1):
        diagonal(q)
    finish(Q - 1)
    diagonal(Q - 1)
    for copy, condition in pending:
        if condition is None:
            copy.wait_send()
        else:
            pl.when(condition)(copy.wait_send)


def body(R, C, inverse_block, factor_cols, diag_inverse, fill_mask):
    rows, cols = factor_cols.shape
    depth = inverse_block.shape[1]
    diag_rows, width = diag_inverse.shape[1:]
    X = max(n for n in range(1, R + 1) if R % n == 0 and n * n <= R)
    Z, G, M = R // X, R // C, C // 2
    halves = cols // LANES
    parts, tiles = split_rows(rows // 2, PARTS), split_rows(rows, TILES)
    Q = 2 * halves
    J = Q * parts
    dma = pltpu.SemaphoreType.DMA
    vmem = pl.BlockSpec(memory_space=pltpu.VMEM)
    return pl.pallas_call(
        functools.partial(kernel, R, C, X),
        out_shape=(
            jax.ShapeDtypeStruct((rows, cols), jnp.bfloat16),
            jax.ShapeDtypeStruct(diag_inverse.shape, jnp.float32),
        ),
        in_specs=[pl.BlockSpec(memory_space=pltpu.SMEM), vmem, vmem, pl.BlockSpec(memory_space=pl.ANY)],
        out_specs=(vmem, vmem),
        scratch_shapes=[
            pltpu.VMEM(inverse_block.shape, jnp.bfloat16),
            pltpu.VMEM((halves, rows, LANES), jnp.bfloat16),
            pltpu.VMEM((Z, Q, rows // 2, LANES), jnp.bfloat16),
            pltpu.VMEM((Q, G, 2, rows // 2, M * LANES), jnp.bfloat16),
            pltpu.VMEM((Q, M, rows, LANES), jnp.float32),
            pltpu.VMEM((Q, M, rows, LANES), jnp.float32),
            pltpu.VMEM((halves, max(M - 1, 1), rows, LANES), jnp.float32),
            pltpu.VMEM((halves, max(M - 1, 1), rows, LANES), jnp.float32),
            pltpu.VMEM((halves, width, LANES), jnp.float32),
            pltpu.VMEM((halves, R - 1, diag_rows, LANES), jnp.float32),
            dma(()), dma((halves,)), dma((halves,)),
            dma((HOPS, 2, Z, J)), dma((Z, J)), dma((Z, J)), dma((G, C, J)),
            dma((max(X - 1, 1), G, J)), dma((G, J)),
            dma((Q, tiles)), dma((Q, tiles)),
            dma((Q, max(M - 1, 1), tiles)), dma((Q, max(M - 1, 1), tiles)),
            dma((halves, R - 1)), dma((halves, R - 1)),
        ],
        compiler_params=pltpu.CompilerParams(
            collective_id=0, has_side_effects=True, vmem_limit_bytes=60 << 20
        ),
        cost_estimate=pl.CostEstimate(
            flops=2 * rows * depth * cols * C, bytes_accessed=2 * rows * depth, transcendentals=0
        ),
    )(fill_mask.T, factor_cols, diag_inverse, inverse_block)


def solution(mesh):
    placed = (P("row", "col"), P("row", "col"), P("col", "row", None), P())
    return jax.shard_map(
        functools.partial(body, mesh.shape["row"], mesh.shape["col"]),
        mesh=mesh,
        in_specs=placed,
        out_specs=(P("row", "col"), P("col", "row", None)),
        check_vma=False,
    )
```

```python
import functools
import math

import jax
import jax.numpy as jnp
from jax import lax
from jax.experimental import pallas as pl
from jax.experimental.pallas import tpu as pltpu
from jax.sharding import PartitionSpec as P

LANES = 128
PARTS = 2
TILES = 4
COPIES = 4
DELAY = 1
HOPS = 1
AHEAD = 1
EARLY = 2
MESH = pl.DeviceIdType.MESH


def split_rows(extent, most):
    return max(n for n in range(1, most + 1) if extent % n == 0 and (extent // n) % 16 == 0)


def kernel(
    R, C, X, mask_ref, factor_ref, diag_ref, a_hbm, out_ref, diag_out_ref,
    a_ref, own_ref, zbuf, fbuf, part, pair_recv, ysend, yrecv, corr, corr_recv,
    a_sem, swap_send, swap_recv, e_send, e_recv, z_send, z_recv, b_send, f_recv, x_send, x_recv,
    p_send, p_recv, y_send, y_recv, c_send, c_recv,
):
    Z, G, M = R // X, R // C, C // 2
    rows, cols = factor_ref.shape
    halves = cols // LANES
    quarters = [(kk, half) for half in range(halves) for kk in range(2)]
    Q = len(quarters)
    width = diag_ref.shape[-1]
    diag_rows = diag_ref.shape[1]
    J, tiles = z_recv.shape[2], p_send.shape[1]
    parts = J // Q
    depth = rows // 2
    pr, mt = depth // parts, rows // tiles
    r, c = lax.axis_index("row"), lax.axis_index("col")
    z, x = r // X, r % X
    m, k = c // 2, c % 2
    partner = m * 2 + 1 - k
    pending = []

    a_copy = pltpu.make_async_copy(a_hbm, a_ref, a_sem)
    a_copy.start()

    barrier = pltpu.get_barrier_semaphore()
    for step in range(1, R):
        pl.semaphore_signal(barrier, inc=1, device_id=((r + step) % R, c), device_id_type=MESH)
    for step in range(1, C):
        pl.semaphore_signal(barrier, inc=1, device_id=(r, (c + step) % C), device_id_type=MESH)

    unit = math.gcd(rows, width)

    def mask_of(index, half):
        block = (r * rows + index * unit) // width
        node = c * (cols // width) + (half * LANES) // width
        return mask_ref[node, block].astype(jnp.float32)

    for half in range(halves):
        for index in range(rows // unit):
            there = pl.ds(index * unit, unit)
            value = factor_ref[there, half * LANES:(half + 1) * LANES].astype(jnp.float32)
            own_ref[half, there, :] = (value * mask_of(index, half)).astype(jnp.bfloat16)

    pl.semaphore_wait(barrier, R - 1 + C - 1)

    def start(copy, condition=None):
        pending.append((copy, condition))
        if condition is None:
            copy.start()
        else:
            pl.when(condition)(copy.start)

    def half_rows(index):
        return pl.ds(pl.multiple_of(index * depth, 16), depth)

    for half in range(halves):
        start(pltpu.make_async_remote_copy(
            src_ref=own_ref.at[half, half_rows(1 - k)], dst_ref=zbuf.at[z, x, half * 2 + k],
            send_sem=swap_send.at[half], recv_sem=swap_recv.at[half],
            device_id=(r, partner), device_id_type=MESH))
    for half in range(halves):
        zbuf[z, x, half * 2 + k] = own_ref[half, half_rows(k), :]

    def place(j):
        return j // parts, pl.ds((j % parts) * pr, pr)

    def early(j):
        return j >= J - EARLY

    def sources(j):
        return [x] + [(x + dx) % X for dx in range(1, X) if early(j)]

    def along_z(plane, xs, j, up, hops, condition):
        q, span = place(j)
        piece = zbuf.at[plane, xs, q, span]
        start(pltpu.make_async_remote_copy(
            src_ref=piece, dst_ref=piece,
            send_sem=z_send.at[hops - 1, 0 if up else 1, plane, xs, j], recv_sem=z_recv.at[plane, xs, j],
            device_id=(r + X * hops if up else r - X * hops, c), device_id_type=MESH), condition)

    def to_owner(plane, xs, j, condition):
        q, span = place(j)
        source = plane * X + xs
        owner, g = source // G, source % G
        dst = fbuf.at[q, g, k, span, pl.ds(pl.multiple_of(m * LANES, LANES), LANES)]
        piece = zbuf.at[plane, xs, q, span]
        here, away = owner == c, owner != c
        if condition is not None:
            here, away = jnp.logical_and(condition, here), jnp.logical_and(condition, away)
        local = pltpu.make_async_copy(piece, dst, f_recv.at[g, c, j])
        pl.when(here)(local.start)
        start(pltpu.make_async_remote_copy(
            src_ref=piece, dst_ref=dst, send_sem=b_send.at[plane, xs, j], recv_sem=f_recv.at[g, c, j],
            device_id=(r, owner), device_id_type=MESH), away)

    def swapped(q):
        kk, half = quarters[q]
        piece = zbuf.at[z, x, q]
        pl.when(k != kk)(pltpu.make_async_copy(piece, piece, swap_recv.at[half]).wait)

    def across(j):
        q, span = place(j)
        for dx in range(1, X):
            piece = zbuf.at[z, x, q, span]
            start(pltpu.make_async_remote_copy(
                src_ref=piece, dst_ref=piece,
                send_sem=e_send.at[dx - 1, j - (J - EARLY)], recv_sem=e_recv.at[x, j - (J - EARLY)],
                device_id=(z * X + (x + dx) % X, c), device_id_type=MESH))

    def own(j):
        q, span = place(j)
        if j % parts == 0 and q not in swaps:
            swapped(q)
            swaps.add(q)
        for xs in sources(j):
            if xs is not x:
                piece = zbuf.at[z, xs, q, span]
                pltpu.make_async_copy(piece, piece, e_recv.at[xs, j - (J - EARLY)]).wait()
            for hops in range(1, HOPS + 1):
                along_z(z, xs, j, True, hops, z + hops < Z)
                along_z(z, xs, j, False, hops, z >= hops)
            to_owner(z, xs, j, None)

    def arrivals(j, d):
        q, span = place(j)
        for xs in sources(j):
            for up in (True, False):
                plane = z - d if up else z + d
                there = z >= d if up else z + d < Z
                safe = jnp.clip(plane, 0, Z - 1)
                piece = zbuf.at[safe, xs, q, span]
                pl.when(there)(pltpu.make_async_copy(piece, piece, z_recv.at[safe, xs, j]).wait)
                if HOPS <= d < Z - 1:
                    onward = z + 1 < Z if up else z > 0
                    along_z(safe, xs, j, up, 1, jnp.logical_and(there, onward))
                to_owner(safe, xs, j, there)

    def collected(g, j):
        q, span = place(j)
        for other in range(C):
            piece = fbuf.at[q, g, other % 2, span, pl.ds(other // 2 * LANES, LANES)]
            pltpu.make_async_copy(piece, piece, f_recv.at[g, other, j]).wait()

    def forward(j):
        if early(j):
            return
        q, span = place(j)
        for g in range(G):
            mine = (G * c + g) % X == x
            whole = fbuf.at[q, g, :, span]

            pl.when(mine)(functools.partial(collected, g, j))
            for dx in range(1, X):
                start(pltpu.make_async_remote_copy(
                    src_ref=whole, dst_ref=whole, send_sem=x_send.at[dx - 1, g, j], recv_sem=x_recv.at[g, j],
                    device_id=(z * X + (x + dx) % X, c), device_id_type=MESH), mine)

    def gather_done(q):
        if q == 0:
            a_copy.wait()
        for p in range(parts):
            j = q * parts + p
            _, span = place(j)
            for g in range(G):
                if early(j):
                    collected(g, j)
                    continue
                whole = fbuf.at[q, g, :, span]
                pl.when((G * c + g) % X != x)(
                    pltpu.make_async_copy(whole, whole, x_recv.at[g, j]).wait)

    def multiply(q, t):
        kk, _ = quarters[q]
        span = pl.ds(t * mt, mt)
        panel = fbuf[q].reshape(G * rows, M * LANES)
        value = jnp.dot(a_ref[span, :], panel, preferred_element_type=jnp.float32)
        for to in range(M):
            part[q, to, span, :] = value[:, to * LANES:(to + 1) * LANES]
        start(pltpu.make_async_remote_copy(
            src_ref=part.at[q, :, span], dst_ref=pair_recv.at[q, :, span],
            send_sem=p_send.at[q, t], recv_sem=p_recv.at[q, t],
            device_id=(r, partner), device_id_type=MESH), k != kk)

    def pair_sum(q, t):
        kk, half = quarters[q]
        span = pl.ds(t * mt, mt)
        piece = pair_recv.at[q, :, span]

        @pl.when(k == kk)
        def _():
            pltpu.make_async_copy(piece, piece, p_recv.at[q, t]).wait()
            for dm in range(1, M):
                to = (m + dm) % M
                ysend[half, dm - 1, span, :] = part[q, to, span, :] + pair_recv[q, to, span, :]

        for dm in range(1, M):
            to = (m + dm) % M
            start(pltpu.make_async_remote_copy(
                src_ref=ysend.at[half, dm - 1, span], dst_ref=yrecv.at[half, dm - 1, span],
                send_sem=y_send.at[q, dm - 1, t], recv_sem=y_recv.at[q, dm - 1, t],
                device_id=(r, to * 2 + k), device_id_type=MESH), k == kk)

    def finish(q):
        kk, half = quarters[q]
        lanes = slice(half * LANES, (half + 1) * LANES)

        @pl.when(k == kk)
        def _():
            for t in range(tiles):
                span = pl.ds(t * mt, mt)
                total = part[q, m, span, :] + pair_recv[q, m, span, :]
                for dm in range(1, M):
                    piece = yrecv.at[half, dm - 1, span]
                    pltpu.make_async_copy(piece, piece, y_recv.at[q, dm - 1, t]).wait()
                    total = total + yrecv[half, dm - 1, span, :]
                part[q, m, span, :] = total
            for index in range(rows // unit):
                there = pl.ds(index * unit, unit)
                value = -part[q, m, there, :] * mask_of(index, half)
                out_ref[there, lanes] = value.astype(jnp.bfloat16)
            for left in range(halves):
                corr[half, left * LANES:(left + 1) * LANES, :] = lax.dot_general(
                    own_ref[left], out_ref[:, lanes], (((0,), (0,)), ((), ())),
                    preferred_element_type=jnp.float32)

        for step in range(1, R):
            to = (r + step) % R
            start(pltpu.make_async_remote_copy(
                src_ref=corr.at[half, pl.ds(pl.multiple_of(to * diag_rows, 8), diag_rows)],
                dst_ref=corr_recv.at[half, step - 1],
                send_sem=c_send.at[half, step - 1], recv_sem=c_recv.at[half, step - 1],
                device_id=(to, c), device_id_type=MESH), k == kk)

    def diagonal(q):
        kk, half = quarters[q]
        lanes = slice(half * LANES, (half + 1) * LANES)

        @pl.when(k == kk)
        def _():
            total = corr[half, pl.ds(pl.multiple_of(r * diag_rows, 8), diag_rows), :]
            for step in range(1, R):
                piece = corr_recv.at[half, step - 1]
                pltpu.make_async_copy(piece, piece, c_recv.at[half, step - 1]).wait()
                total = total + corr_recv[half, step - 1]
            diag_out_ref[0, :, lanes] = diag_ref[0, :, lanes] - total

    def work(q):
        def first():
            gather_done(q)
            multiply(q, 0)

        def sums():
            for t in range(tiles):
                pair_sum(q, t)

        jobs = [first] + [functools.partial(multiply, q, t) for t in range(1, tiles)] + [sums]
        if q >= 1:
            jobs.append(functools.partial(finish, q - 1))
        return jobs

    swaps = set()
    for j in range(min(AHEAD, J)):
        own(j)
    for j in range(J - EARLY, J):
        if j // parts not in swaps:
            swapped(j // parts)
            swaps.add(j // parts)
        across(j)
    jobs, done = [], 0
    for j in range(J):
        for d in range(1, Z):
            arrivals(j, d)
            if d == 1 and j + AHEAD < J:
                own(j + AHEAD)
            if jobs:
                jobs.pop(0)()
        if j >= 1:
            forward(j - 1)
        if j - DELAY >= (done + 1) * parts:
            jobs += work(done)
            done += 1
    forward(J - 1)
    for job in jobs:
        job()
    for q in range(done, Q):
        gather_done(q)
        for t in range(tiles):
            multiply(q, t)
            if t >= 1:
                pair_sum(q, t - 1)
        pair_sum(q, tiles - 1)
        if q >= 1:
            finish(q - 1)
    for q in range(Q - 1):
        diagonal(q)
    finish(Q - 1)
    diagonal(Q - 1)
    for copy, condition in pending:
        if condition is None:
            copy.wait_send()
        else:
            pl.when(condition)(copy.wait_send)


def hand_over(cols_ref, diag_ref, cols_out, diag_out, sems):
    rows = cols_ref.shape[0] // COPIES
    copies = [pltpu.make_async_copy(diag_ref, diag_out, sems.at[COPIES])]
    for n in range(COPIES):
        span = pl.ds(n * rows, rows)
        copies.append(pltpu.make_async_copy(cols_ref.at[span], cols_out.at[span], sems.at[n]))
    for copy in copies:
        copy.start()
    for copy in copies:
        copy.wait()


def body(R, C, inverse_block, factor_cols, diag_inverse, fill_mask):
    rows, cols = factor_cols.shape
    depth = inverse_block.shape[1]
    diag_rows, width = diag_inverse.shape[1:]
    X = max(n for n in range(1, R + 1) if R % n == 0 and n * n <= R)
    Z, G, M = R // X, R // C, C // 2
    halves = cols // LANES
    parts, tiles = split_rows(rows // 2, PARTS), split_rows(rows, TILES)
    Q = 2 * halves
    J = Q * parts
    dma = pltpu.SemaphoreType.DMA
    vmem = pl.BlockSpec(memory_space=pltpu.VMEM)
    out_shape = (
        jax.ShapeDtypeStruct((rows, cols), jnp.bfloat16),
        jax.ShapeDtypeStruct(diag_inverse.shape, jnp.float32),
    )
    results = pl.pallas_call(
        functools.partial(kernel, R, C, X),
        out_shape=out_shape,
        in_specs=[pl.BlockSpec(memory_space=pltpu.SMEM), vmem, vmem, pl.BlockSpec(memory_space=pl.ANY)],
        out_specs=(vmem, vmem),
        scratch_shapes=[
            pltpu.VMEM(inverse_block.shape, jnp.bfloat16),
            pltpu.VMEM((halves, rows, LANES), jnp.bfloat16),
            pltpu.VMEM((Z, X, Q, rows // 2, LANES), jnp.bfloat16),
            pltpu.VMEM((Q, G, 2, rows // 2, M * LANES), jnp.bfloat16),
            pltpu.VMEM((Q, M, rows, LANES), jnp.float32),
            pltpu.VMEM((Q, M, rows, LANES), jnp.float32),
            pltpu.VMEM((halves, max(M - 1, 1), rows, LANES), jnp.float32),
            pltpu.VMEM((halves, max(M - 1, 1), rows, LANES), jnp.float32),
            pltpu.VMEM((halves, width, LANES), jnp.float32),
            pltpu.VMEM((halves, R - 1, diag_rows, LANES), jnp.float32),
            dma(()), dma((halves,)), dma((halves,)),
            dma((max(X - 1, 1), EARLY)), dma((X, EARLY)),
            dma((HOPS, 2, Z, X, J)), dma((Z, X, J)), dma((Z, X, J)), dma((G, C, J)),
            dma((max(X - 1, 1), G, J)), dma((G, J)),
            dma((Q, tiles)), dma((Q, tiles)),
            dma((Q, max(M - 1, 1), tiles)), dma((Q, max(M - 1, 1), tiles)),
            dma((halves, R - 1)), dma((halves, R - 1)),
        ],
        compiler_params=pltpu.CompilerParams(
            collective_id=0, has_side_effects=True, vmem_limit_bytes=60 << 20
        ),
        cost_estimate=pl.CostEstimate(
            flops=2 * rows * depth * cols * C, bytes_accessed=2 * rows * depth, transcendentals=0
        ),
    )(fill_mask.T, factor_cols, diag_inverse, inverse_block)
    anywhere = pl.BlockSpec(memory_space=pl.ANY)
    return pl.pallas_call(
        hand_over,
        out_shape=out_shape,
        in_specs=[anywhere, anywhere],
        out_specs=(anywhere, anywhere),
        scratch_shapes=[dma((COPIES + 1,))],
    )(*results)


def solution(mesh):
    placed = (P("row", "col"), P("row", "col"), P("col", "row", None), P())
    return jax.shard_map(
        functools.partial(body, mesh.shape["row"], mesh.shape["col"]),
        mesh=mesh,
        in_specs=placed,
        out_specs=(P("row", "col"), P("col", "row", None)),
        check_vma=False,
    )
```

```python
import functools
import math

import jax
import jax.numpy as jnp
from jax import lax
from jax.experimental import pallas as pl
from jax.experimental.pallas import tpu as pltpu
from jax.sharding import PartitionSpec as P

LANES = 128
PARTS = 2
TILES = 5
DELAY = 1
HOPS = 1
AHEAD = 1
EARLY = 1
MESH = pl.DeviceIdType.MESH


def split_rows(extent, most):
    return max(n for n in range(1, most + 1) if extent % n == 0 and (extent // n) % 16 == 0)


def kernel(
    R, C, X, mask_ref, factor_ref, diag_ref, a_hbm, out_ref, diag_out_ref,
    a_ref, own_ref, zbuf, fbuf, part, pair_recv, ysend, yrecv, corr, corr_recv,
    a_sem, swap_send, swap_recv, e_send, e_recv, z_send, z_recv, b_send, f_recv, x_send, x_recv,
    p_send, p_recv, y_send, y_recv, c_send, c_recv,
):
    Z, G, M = R // X, R // C, C // 2
    rows, cols = factor_ref.shape
    halves = cols // LANES
    quarters = [(kk, half) for half in range(halves) for kk in range(2)]
    Q = len(quarters)
    width = diag_ref.shape[-1]
    diag_rows = diag_ref.shape[1]
    J, tiles = z_recv.shape[2], p_send.shape[1]
    parts = J // Q
    depth = rows // 2
    pr, mt = depth // parts, rows // tiles
    r, c = lax.axis_index("row"), lax.axis_index("col")
    z, x = r // X, r % X
    m, k = c // 2, c % 2
    partner = m * 2 + 1 - k
    pending = []

    a_copy = pltpu.make_async_copy(a_hbm, a_ref, a_sem)
    a_copy.start()

    barrier = pltpu.get_barrier_semaphore()
    for step in range(1, R):
        pl.semaphore_signal(barrier, inc=1, device_id=((r + step) % R, c), device_id_type=MESH)
    for step in range(1, C):
        pl.semaphore_signal(barrier, inc=1, device_id=(r, (c + step) % C), device_id_type=MESH)

    unit = math.gcd(rows, width)

    def mask_of(index, half):
        block = (r * rows + index * unit) // width
        node = c * (cols // width) + (half * LANES) // width
        return mask_ref[node, block].astype(jnp.float32)

    for half in range(halves):
        for index in range(rows // unit):
            there = pl.ds(index * unit, unit)
            value = factor_ref[there, half * LANES:(half + 1) * LANES].astype(jnp.float32)
            own_ref[half, there, :] = (value * mask_of(index, half)).astype(jnp.bfloat16)

    pl.semaphore_wait(barrier, R - 1 + C - 1)

    def start(copy, condition=None):
        pending.append((copy, condition))
        if condition is None:
            copy.start()
        else:
            pl.when(condition)(copy.start)

    def half_rows(index):
        return pl.ds(pl.multiple_of(index * depth, 16), depth)

    for half in range(halves):
        start(pltpu.make_async_remote_copy(
            src_ref=own_ref.at[half, half_rows(1 - k)], dst_ref=zbuf.at[z, x, half * 2 + k],
            send_sem=swap_send.at[half], recv_sem=swap_recv.at[half],
            device_id=(r, partner), device_id_type=MESH))
    for half in range(halves):
        zbuf[z, x, half * 2 + k] = own_ref[half, half_rows(k), :]

    def place(j):
        return j // parts, pl.ds((j % parts) * pr, pr)

    def early(j):
        return j >= J - EARLY

    def sources(j):
        return [x] + [(x + dx) % X for dx in range(1, X) if early(j)]

    def along_z(plane, xs, j, up, hops, condition):
        q, span = place(j)
        piece = zbuf.at[plane, xs, q, span]
        start(pltpu.make_async_remote_copy(
            src_ref=piece, dst_ref=piece,
            send_sem=z_send.at[hops - 1, 0 if up else 1, plane, xs, j], recv_sem=z_recv.at[plane, xs, j],
            device_id=(r + X * hops if up else r - X * hops, c), device_id_type=MESH), condition)

    def to_owner(plane, xs, j, condition):
        q, span = place(j)
        source = plane * X + xs
        owner, g = source // G, source % G
        dst = fbuf.at[q, g, k, span, pl.ds(pl.multiple_of(m * LANES, LANES), LANES)]
        piece = zbuf.at[plane, xs, q, span]
        here, away = owner == c, owner != c
        if condition is not None:
            here, away = jnp.logical_and(condition, here), jnp.logical_and(condition, away)
        local = pltpu.make_async_copy(piece, dst, f_recv.at[g, c, j])
        pl.when(here)(local.start)
        start(pltpu.make_async_remote_copy(
            src_ref=piece, dst_ref=dst, send_sem=b_send.at[plane, xs, j], recv_sem=f_recv.at[g, c, j],
            device_id=(r, owner), device_id_type=MESH), away)

    def swapped(q):
        kk, half = quarters[q]
        piece = zbuf.at[z, x, q]
        pl.when(k != kk)(pltpu.make_async_copy(piece, piece, swap_recv.at[half]).wait)

    def across(j):
        q, span = place(j)
        for dx in range(1, X):
            piece = zbuf.at[z, x, q, span]
            start(pltpu.make_async_remote_copy(
                src_ref=piece, dst_ref=piece,
                send_sem=e_send.at[dx - 1, j - (J - EARLY)], recv_sem=e_recv.at[x, j - (J - EARLY)],
                device_id=(z * X + (x + dx) % X, c), device_id_type=MESH))

    def own(j):
        q, span = place(j)
        if j % parts == 0 and q not in swaps:
            swapped(q)
            swaps.add(q)
        for xs in sources(j):
            if xs is not x:
                piece = zbuf.at[z, xs, q, span]
                pltpu.make_async_copy(piece, piece, e_recv.at[xs, j - (J - EARLY)]).wait()
            for hops in range(1, HOPS + 1):
                along_z(z, xs, j, True, hops, z + hops < Z)
                along_z(z, xs, j, False, hops, z >= hops)
            to_owner(z, xs, j, None)

    def arrivals(j, d):
        q, span = place(j)
        for xs in sources(j):
            for up in (True, False):
                plane = z - d if up else z + d
                there = z >= d if up else z + d < Z
                safe = jnp.clip(plane, 0, Z - 1)
                piece = zbuf.at[safe, xs, q, span]
                pl.when(there)(pltpu.make_async_copy(piece, piece, z_recv.at[safe, xs, j]).wait)
                if HOPS <= d < Z - 1:
                    onward = z + 1 < Z if up else z > 0
                    along_z(safe, xs, j, up, 1, jnp.logical_and(there, onward))
                to_owner(safe, xs, j, there)

    def collected(g, j):
        q, span = place(j)
        for other in range(C):
            piece = fbuf.at[q, g, other % 2, span, pl.ds(other // 2 * LANES, LANES)]
            pltpu.make_async_copy(piece, piece, f_recv.at[g, other, j]).wait()

    def forward(j):
        if early(j):
            return
        q, span = place(j)
        for g in range(G):
            mine = (G * c + g) % X == x
            whole = fbuf.at[q, g, :, span]

            pl.when(mine)(functools.partial(collected, g, j))
            for dx in range(1, X):
                start(pltpu.make_async_remote_copy(
                    src_ref=whole, dst_ref=whole, send_sem=x_send.at[dx - 1, g, j], recv_sem=x_recv.at[g, j],
                    device_id=(z * X + (x + dx) % X, c), device_id_type=MESH), mine)

    def gather_done(q, begun=False):
        if q == 0:
            a_copy.wait()
        for p in range(parts):
            j = q * parts + p
            _, span = place(j)
            for g in range(G):
                if early(j):
                    if begun:
                        pl.when(jnp.logical_not(mine(g)))(functools.partial(collected, g, j))
                    else:
                        collected(g, j)
                    continue
                whole = fbuf.at[q, g, :, span]
                pl.when((G * c + g) % X != x)(
                    pltpu.make_async_copy(whole, whole, x_recv.at[g, j]).wait)

    def mine(g):
        return (G * c + g) % X == x

    def add_group(q, g, t):
        span = pl.ds(t * mt, mt)
        panel = fbuf[q, g].reshape(rows, M * LANES)
        value = jnp.dot(a_ref[span, g * rows:(g + 1) * rows], panel, preferred_element_type=jnp.float32)
        for to in range(M):
            part[q, to, span, :] += value[:, to * LANES:(to + 1) * LANES]

    def begin(q):
        part[q] = jnp.zeros(part.shape[1:], jnp.float32)
        for g in range(G):
            @pl.when(mine(g))
            def _():
                for p in range(parts):
                    if early(q * parts + p):
                        collected(g, q * parts + p)
                for t in range(tiles):
                    add_group(q, g, t)

    def complete(q, t):
        for g in range(G):
            pl.when(jnp.logical_not(mine(g)))(functools.partial(add_group, q, g, t))
        send_pair(q, t)

    def send_pair(q, t):
        kk, _ = quarters[q]
        span = pl.ds(t * mt, mt)
        start(pltpu.make_async_remote_copy(
            src_ref=part.at[q, :, span], dst_ref=pair_recv.at[q, :, span],
            send_sem=p_send.at[q, t], recv_sem=p_recv.at[q, t],
            device_id=(r, partner), device_id_type=MESH), k != kk)

    def multiply(q, t):
        span = pl.ds(t * mt, mt)
        panel = fbuf[q].reshape(G * rows, M * LANES)
        value = jnp.dot(a_ref[span, :], panel, preferred_element_type=jnp.float32)
        for to in range(M):
            part[q, to, span, :] = value[:, to * LANES:(to + 1) * LANES]
        send_pair(q, t)

    def pair_sum(q, t):
        kk, half = quarters[q]
        span = pl.ds(t * mt, mt)
        piece = pair_recv.at[q, :, span]

        @pl.when(k == kk)
        def _():
            pltpu.make_async_copy(piece, piece, p_recv.at[q, t]).wait()
            for dm in range(1, M):
                to = (m + dm) % M
                ysend[half, dm - 1, span, :] = part[q, to, span, :] + pair_recv[q, to, span, :]

        for dm in range(1, M):
            to = (m + dm) % M
            start(pltpu.make_async_remote_copy(
                src_ref=ysend.at[half, dm - 1, span], dst_ref=yrecv.at[half, dm - 1, span],
                send_sem=y_send.at[q, dm - 1, t], recv_sem=y_recv.at[q, dm - 1, t],
                device_id=(r, to * 2 + k), device_id_type=MESH), k == kk)

    def finish(q):
        kk, half = quarters[q]
        lanes = slice(half * LANES, (half + 1) * LANES)

        @pl.when(k == kk)
        def _():
            for t in range(tiles):
                span = pl.ds(t * mt, mt)
                total = part[q, m, span, :] + pair_recv[q, m, span, :]
                for dm in range(1, M):
                    piece = yrecv.at[half, dm - 1, span]
                    pltpu.make_async_copy(piece, piece, y_recv.at[q, dm - 1, t]).wait()
                    total = total + yrecv[half, dm - 1, span, :]
                for index in range(mt // unit):
                    value = -total[index * unit:(index + 1) * unit] * mask_of(t * (mt // unit) + index, half)
                    out_ref[pl.ds(t * mt + index * unit, unit), lanes] = value.astype(jnp.bfloat16)
                for left in range(halves):
                    there = slice(left * LANES, (left + 1) * LANES)
                    product = lax.dot_general(
                        own_ref[left, span, :], out_ref[span, lanes], (((0,), (0,)), ((), ())),
                        preferred_element_type=jnp.float32)
                    if t == 0:
                        corr[half, there, :] = product
                    else:
                        corr[half, there, :] += product

        for step in range(1, R):
            to = (r + step) % R
            start(pltpu.make_async_remote_copy(
                src_ref=corr.at[half, pl.ds(pl.multiple_of(to * diag_rows, 8), diag_rows)],
                dst_ref=corr_recv.at[half, step - 1],
                send_sem=c_send.at[half, step - 1], recv_sem=c_recv.at[half, step - 1],
                device_id=(to, c), device_id_type=MESH), k == kk)

    def diagonal(q):
        kk, half = quarters[q]
        lanes = slice(half * LANES, (half + 1) * LANES)

        @pl.when(k == kk)
        def _():
            total = corr[half, pl.ds(pl.multiple_of(r * diag_rows, 8), diag_rows), :]
            for step in range(1, R):
                piece = corr_recv.at[half, step - 1]
                pltpu.make_async_copy(piece, piece, c_recv.at[half, step - 1]).wait()
                total = total + corr_recv[half, step - 1]
            diag_out_ref[0, :, lanes] = diag_ref[0, :, lanes] - total

    def work(q):
        def first():
            gather_done(q)
            multiply(q, 0)

        def sums():
            for t in range(tiles):
                pair_sum(q, t)

        jobs = [first] + [functools.partial(multiply, q, t) for t in range(1, tiles)] + [sums]
        if q >= 1:
            jobs.append(functools.partial(finish, q - 1))
        return jobs

    swaps = set()
    for j in range(min(AHEAD, J)):
        own(j)
    for j in range(J - EARLY, J):
        if j // parts not in swaps:
            swapped(j // parts)
            swaps.add(j // parts)
        across(j)
    jobs, done = [], 0
    for j in range(J):
        for d in range(1, Z):
            arrivals(j, d)
            if d == 1 and j + AHEAD < J:
                own(j + AHEAD)
            if d == max(Z - 2, 1) and j >= 1:
                forward(j - 1)
            if jobs:
                jobs.pop(0)()
        if j - DELAY >= (done + 1) * parts:
            jobs += work(done)
            done += 1
    forward(J - 1)
    for job in jobs:
        job()
    for q in range(done, Q):
        last = q == Q - 1 and q > 0
        if last:
            begin(q)
        gather_done(q, last)
        for t in range(tiles):
            (complete if last else multiply)(q, t)
            if t >= 1:
                pair_sum(q, t - 1)
        pair_sum(q, tiles - 1)
        if q >= 1:
            finish(q - 1)
    for q in range(Q - 1):
        diagonal(q)
    finish(Q - 1)
    diagonal(Q - 1)
    for copy, condition in pending:
        if condition is None:
            copy.wait_send()
        else:
            pl.when(condition)(copy.wait_send)


def hand_over(cols_ref, diag_ref, cols_out, diag_out):
    cols_out[...] = cols_ref[...]
    diag_out[...] = diag_ref[...]


def body(R, C, inverse_block, factor_cols, diag_inverse, fill_mask):
    rows, cols = factor_cols.shape
    depth = inverse_block.shape[1]
    diag_rows, width = diag_inverse.shape[1:]
    X = max(n for n in range(1, R + 1) if R % n == 0 and n * n <= R)
    Z, G, M = R // X, R // C, C // 2
    halves = cols // LANES
    parts = split_rows(rows // 2, PARTS)
    blocks = rows // math.gcd(rows, width)
    tiles = max(n for n in range(1, TILES + 1) if blocks % n == 0)
    Q = 2 * halves
    J = Q * parts
    dma = pltpu.SemaphoreType.DMA
    vmem = pl.BlockSpec(memory_space=pltpu.VMEM)
    out_shape = (
        jax.ShapeDtypeStruct((rows, cols), jnp.bfloat16),
        jax.ShapeDtypeStruct(diag_inverse.shape, jnp.float32),
    )
    results = pl.pallas_call(
        functools.partial(kernel, R, C, X),
        out_shape=out_shape,
        in_specs=[pl.BlockSpec(memory_space=pltpu.SMEM), vmem, vmem, pl.BlockSpec(memory_space=pl.ANY)],
        out_specs=(vmem, vmem),
        scratch_shapes=[
            pltpu.VMEM(inverse_block.shape, jnp.bfloat16),
            pltpu.VMEM((halves, rows, LANES), jnp.bfloat16),
            pltpu.VMEM((Z, X, Q, rows // 2, LANES), jnp.bfloat16),
            pltpu.VMEM((Q, G, 2, rows // 2, M * LANES), jnp.bfloat16),
            pltpu.VMEM((Q, M, rows, LANES), jnp.float32),
            pltpu.VMEM((Q, M, rows, LANES), jnp.float32),
            pltpu.VMEM((halves, max(M - 1, 1), rows, LANES), jnp.float32),
            pltpu.VMEM((halves, max(M - 1, 1), rows, LANES), jnp.float32),
            pltpu.VMEM((halves, width, LANES), jnp.float32),
            pltpu.VMEM((halves, R - 1, diag_rows, LANES), jnp.float32),
            dma(()), dma((halves,)), dma((halves,)),
            dma((max(X - 1, 1), EARLY)), dma((X, EARLY)),
            dma((HOPS, 2, Z, X, J)), dma((Z, X, J)), dma((Z, X, J)), dma((G, C, J)),
            dma((max(X - 1, 1), G, J)), dma((G, J)),
            dma((Q, tiles)), dma((Q, tiles)),
            dma((Q, max(M - 1, 1), tiles)), dma((Q, max(M - 1, 1), tiles)),
            dma((halves, R - 1)), dma((halves, R - 1)),
        ],
        compiler_params=pltpu.CompilerParams(
            collective_id=0, has_side_effects=True, vmem_limit_bytes=60 << 20
        ),
        cost_estimate=pl.CostEstimate(
            flops=2 * rows * depth * cols * C, bytes_accessed=2 * rows * depth, transcendentals=0
        ),
    )(fill_mask.T, factor_cols, diag_inverse, inverse_block)
    return pl.pallas_call(
        hand_over,
        out_shape=out_shape,
        in_specs=[vmem, vmem],
        out_specs=(vmem, vmem),
    )(*results)


def solution(mesh):
    placed = (P("row", "col"), P("row", "col"), P("col", "row", None), P())
    return jax.shard_map(
        functools.partial(body, mesh.shape["row"], mesh.shape["col"]),
        mesh=mesh,
        in_specs=placed,
        out_specs=(P("row", "col"), P("col", "row", None)),
        check_vma=False,
    )
```

```python
import functools
import math

import jax
import jax.numpy as jnp
from jax import lax
from jax.experimental import pallas as pl
from jax.experimental.pallas import tpu as pltpu
from jax.sharding import PartitionSpec as P

LANES = 128
PARTS = 4
TILES = 5
DELAY = 2
HOPS = 1
AHEAD = 1
EARLY = 2
MESH = pl.DeviceIdType.MESH


def split_rows(extent, most):
    return max(n for n in range(1, most + 1) if extent % n == 0 and (extent // n) % 16 == 0)


def kernel(
    R, C, X, mask_ref, factor_ref, diag_ref, a_hbm, out_ref, diag_out_ref,
    a_ref, own_ref, zbuf, fbuf, part, pair_recv, ysend, yrecv, corr, corr_recv,
    a_sem, swap_send, swap_recv, e_send, e_recv, z_send, z_recv, b_send, f_recv, x_send, x_recv,
    p_send, p_recv, y_send, y_recv, c_send, c_recv,
):
    Z, G, M = R // X, R // C, C // 2
    rows, cols = factor_ref.shape
    halves = cols // LANES
    quarters = [(kk, half) for half in range(halves) for kk in range(2)]
    Q = len(quarters)
    width = diag_ref.shape[-1]
    diag_rows = diag_ref.shape[1]
    J, tiles = z_recv.shape[2], p_send.shape[1]
    parts = J // Q
    depth = rows // 2
    pr, mt = depth // parts, rows // tiles
    r, c = lax.axis_index("row"), lax.axis_index("col")
    z, x = r // X, r % X
    m, k = c // 2, c % 2
    partner = m * 2 + 1 - k
    pending = []

    a_copy = pltpu.make_async_copy(a_hbm, a_ref, a_sem)
    a_copy.start()

    barrier = pltpu.get_barrier_semaphore()
    for step in range(1, R):
        pl.semaphore_signal(barrier, inc=1, device_id=((r + step) % R, c), device_id_type=MESH)
    for step in range(1, C):
        pl.semaphore_signal(barrier, inc=1, device_id=(r, (c + step) % C), device_id_type=MESH)

    unit = math.gcd(rows, width)

    def mask_of(index, half):
        block = (r * rows + index * unit) // width
        node = c * (cols // width) + (half * LANES) // width
        return mask_ref[node, block].astype(jnp.float32)

    for half in range(halves):
        for index in range(rows // unit):
            there = pl.ds(index * unit, unit)
            value = factor_ref[there, half * LANES:(half + 1) * LANES].astype(jnp.float32)
            own_ref[half, there, :] = (value * mask_of(index, half)).astype(jnp.bfloat16)

    pl.semaphore_wait(barrier, R - 1 + C - 1)

    def start(copy, condition=None):
        pending.append((copy, condition))
        if condition is None:
            copy.start()
        else:
            pl.when(condition)(copy.start)

    def half_rows(index):
        return pl.ds(pl.multiple_of(index * depth, 16), depth)

    for half in range(halves):
        start(pltpu.make_async_remote_copy(
            src_ref=own_ref.at[half, half_rows(1 - k)], dst_ref=zbuf.at[z, x, half * 2 + k],
            send_sem=swap_send.at[half], recv_sem=swap_recv.at[half],
            device_id=(r, partner), device_id_type=MESH))
    for half in range(halves):
        zbuf[z, x, half * 2 + k] = own_ref[half, half_rows(k), :]

    def place(j):
        return j // parts, pl.ds((j % parts) * pr, pr)

    def early(j):
        return j >= J - EARLY

    def sources(j):
        return [x] + [(x + dx) % X for dx in range(1, X) if early(j)]

    def along_z(plane, xs, j, up, hops, condition):
        q, span = place(j)
        piece = zbuf.at[plane, xs, q, span]
        start(pltpu.make_async_remote_copy(
            src_ref=piece, dst_ref=piece,
            send_sem=z_send.at[hops - 1, 0 if up else 1, plane, xs, j], recv_sem=z_recv.at[plane, xs, j],
            device_id=(r + X * hops if up else r - X * hops, c), device_id_type=MESH), condition)

    def to_owner(plane, xs, j, condition):
        q, span = place(j)
        source = plane * X + xs
        owner, g = source // G, source % G
        dst = fbuf.at[q, g, k, span, pl.ds(pl.multiple_of(m * LANES, LANES), LANES)]
        piece = zbuf.at[plane, xs, q, span]
        here, away = owner == c, owner != c
        if condition is not None:
            here, away = jnp.logical_and(condition, here), jnp.logical_and(condition, away)
        local = pltpu.make_async_copy(piece, dst, f_recv.at[g, c, j])
        pl.when(here)(local.start)
        start(pltpu.make_async_remote_copy(
            src_ref=piece, dst_ref=dst, send_sem=b_send.at[plane, xs, j], recv_sem=f_recv.at[g, c, j],
            device_id=(r, owner), device_id_type=MESH), away)

    def swapped(q):
        kk, half = quarters[q]
        piece = zbuf.at[z, x, q]
        pl.when(k != kk)(pltpu.make_async_copy(piece, piece, swap_recv.at[half]).wait)

    def across(j):
        q, span = place(j)
        for dx in range(1, X):
            piece = zbuf.at[z, x, q, span]
            start(pltpu.make_async_remote_copy(
                src_ref=piece, dst_ref=piece,
                send_sem=e_send.at[dx - 1, j - (J - EARLY)], recv_sem=e_recv.at[x, j - (J - EARLY)],
                device_id=(z * X + (x + dx) % X, c), device_id_type=MESH))

    def own(j):
        q, span = place(j)
        if j % parts == 0 and q not in swaps:
            swapped(q)
            swaps.add(q)
        for xs in sources(j):
            if xs is not x:
                piece = zbuf.at[z, xs, q, span]
                pltpu.make_async_copy(piece, piece, e_recv.at[xs, j - (J - EARLY)]).wait()
            for hops in range(1, HOPS + 1):
                along_z(z, xs, j, True, hops, z + hops < Z)
                along_z(z, xs, j, False, hops, z >= hops)
            to_owner(z, xs, j, None)

    def arrivals(j, d):
        q, span = place(j)
        for xs in sources(j):
            for up in (True, False):
                plane = z - d if up else z + d
                there = z >= d if up else z + d < Z
                safe = jnp.clip(plane, 0, Z - 1)
                piece = zbuf.at[safe, xs, q, span]
                pl.when(there)(pltpu.make_async_copy(piece, piece, z_recv.at[safe, xs, j]).wait)
                if HOPS <= d < Z - 1:
                    onward = z + 1 < Z if up else z > 0
                    along_z(safe, xs, j, up, 1, jnp.logical_and(there, onward))
                to_owner(safe, xs, j, there)

    def collected(g, j):
        q, span = place(j)
        for other in range(C):
            piece = fbuf.at[q, g, other % 2, span, pl.ds(other // 2 * LANES, LANES)]
            pltpu.make_async_copy(piece, piece, f_recv.at[g, other, j]).wait()

    def forward(j):
        if early(j):
            return
        q, span = place(j)
        for g in range(G):
            mine = (G * c + g) % X == x
            whole = fbuf.at[q, g, :, span]

            pl.when(mine)(functools.partial(collected, g, j))
            for dx in range(1, X):
                start(pltpu.make_async_remote_copy(
                    src_ref=whole, dst_ref=whole, send_sem=x_send.at[dx - 1, g, j], recv_sem=x_recv.at[g, j],
                    device_id=(z * X + (x + dx) % X, c), device_id_type=MESH), mine)

    def gather_done(q, begun=False):
        if q == 0:
            a_copy.wait()
        for p in range(parts):
            j = q * parts + p
            _, span = place(j)
            for g in range(G):
                if early(j):
                    if begun:
                        pl.when(jnp.logical_not(mine(g)))(functools.partial(collected, g, j))
                    else:
                        collected(g, j)
                    continue
                whole = fbuf.at[q, g, :, span]
                pl.when((G * c + g) % X != x)(
                    pltpu.make_async_copy(whole, whole, x_recv.at[g, j]).wait)

    def mine(g):
        return (G * c + g) % X == x

    def add_group(q, g, t):
        span = pl.ds(t * mt, mt)
        panel = fbuf[q, g].reshape(rows, M * LANES)
        value = jnp.dot(a_ref[span, g * rows:(g + 1) * rows], panel, preferred_element_type=jnp.float32)
        for to in range(M):
            part[q, to, span, :] += value[:, to * LANES:(to + 1) * LANES]

    def begin(q):
        part[q] = jnp.zeros(part.shape[1:], jnp.float32)
        for g in range(G):
            @pl.when(mine(g))
            def _():
                for p in range(parts):
                    if early(q * parts + p):
                        collected(g, q * parts + p)
                for t in range(tiles):
                    add_group(q, g, t)

    def complete(q, t):
        for g in range(G):
            pl.when(jnp.logical_not(mine(g)))(functools.partial(add_group, q, g, t))
        send_pair(q, t)

    def send_pair(q, t):
        kk, _ = quarters[q]
        span = pl.ds(t * mt, mt)
        start(pltpu.make_async_remote_copy(
            src_ref=part.at[q, :, span], dst_ref=pair_recv.at[q, :, span],
            send_sem=p_send.at[q, t], recv_sem=p_recv.at[q, t],
            device_id=(r, partner), device_id_type=MESH), k != kk)

    def multiply(q, t):
        span = pl.ds(t * mt, mt)
        panel = fbuf[q].reshape(G * rows, M * LANES)
        value = jnp.dot(a_ref[span, :], panel, preferred_element_type=jnp.float32)
        for to in range(M):
            part[q, to, span, :] = value[:, to * LANES:(to + 1) * LANES]
        send_pair(q, t)

    def pair_sum(q, t):
        kk, half = quarters[q]
        span = pl.ds(t * mt, mt)
        piece = pair_recv.at[q, :, span]

        @pl.when(k == kk)
        def _():
            pltpu.make_async_copy(piece, piece, p_recv.at[q, t]).wait()
            for dm in range(1, M):
                to = (m + dm) % M
                ysend[half, dm - 1, span, :] = part[q, to, span, :] + pair_recv[q, to, span, :]

        for dm in range(1, M):
            to = (m + dm) % M
            start(pltpu.make_async_remote_copy(
                src_ref=ysend.at[half, dm - 1, span], dst_ref=yrecv.at[half, dm - 1, span],
                send_sem=y_send.at[q, dm - 1, t], recv_sem=y_recv.at[q, dm - 1, t],
                device_id=(r, to * 2 + k), device_id_type=MESH), k == kk)

    def finish(q):
        kk, half = quarters[q]
        lanes = slice(half * LANES, (half + 1) * LANES)

        @pl.when(k == kk)
        def _():
            for t in range(tiles):
                span = pl.ds(t * mt, mt)
                total = part[q, m, span, :] + pair_recv[q, m, span, :]
                for dm in range(1, M):
                    piece = yrecv.at[half, dm - 1, span]
                    pltpu.make_async_copy(piece, piece, y_recv.at[q, dm - 1, t]).wait()
                    total = total + yrecv[half, dm - 1, span, :]
                for index in range(mt // unit):
                    value = -total[index * unit:(index + 1) * unit] * mask_of(t * (mt // unit) + index, half)
                    out_ref[pl.ds(t * mt + index * unit, unit), lanes] = value.astype(jnp.bfloat16)
                for left in range(halves):
                    there = slice(left * LANES, (left + 1) * LANES)
                    product = lax.dot_general(
                        own_ref[left, span, :], out_ref[span, lanes], (((0,), (0,)), ((), ())),
                        preferred_element_type=jnp.float32)
                    if t == 0:
                        corr[half, there, :] = product
                    else:
                        corr[half, there, :] += product

        for step in range(1, R):
            to = (r + step) % R
            start(pltpu.make_async_remote_copy(
                src_ref=corr.at[half, pl.ds(pl.multiple_of(to * diag_rows, 8), diag_rows)],
                dst_ref=corr_recv.at[half, step - 1],
                send_sem=c_send.at[half, step - 1], recv_sem=c_recv.at[half, step - 1],
                device_id=(to, c), device_id_type=MESH), k == kk)

    def diagonal(q):
        kk, half = quarters[q]
        lanes = slice(half * LANES, (half + 1) * LANES)

        @pl.when(k == kk)
        def _():
            total = corr[half, pl.ds(pl.multiple_of(r * diag_rows, 8), diag_rows), :]
            for step in range(1, R):
                piece = corr_recv.at[half, step - 1]
                pltpu.make_async_copy(piece, piece, c_recv.at[half, step - 1]).wait()
                total = total + corr_recv[half, step - 1]
            diag_out_ref[0, :, lanes] = diag_ref[0, :, lanes] - total

    def work(q):
        def first():
            gather_done(q)
            multiply(q, 0)

        def sums():
            for t in range(tiles):
                pair_sum(q, t)

        jobs = [first] + [functools.partial(multiply, q, t) for t in range(1, tiles)] + [sums]
        if q >= 1:
            jobs.append(functools.partial(finish, q - 1))
        return jobs

    swaps = set()
    for j in range(min(AHEAD, J)):
        own(j)
    for j in range(J - EARLY, J):
        if j // parts not in swaps:
            swapped(j // parts)
            swaps.add(j // parts)
        across(j)
    jobs, done = [], 0
    for j in range(J):
        for d in range(1, Z):
            arrivals(j, d)
            if d == 1 and j + AHEAD < J:
                own(j + AHEAD)
            if d == max(Z - 2, 1) and j >= 1:
                forward(j - 1)
            if jobs:
                jobs.pop(0)()
        if j - DELAY >= (done + 1) * parts:
            jobs += work(done)
            done += 1
    forward(J - 1)
    for job in jobs:
        job()
    for q in range(done, Q):
        last = q == Q - 1 and q > 0
        if last:
            begin(q)
        gather_done(q, last)
        for t in range(tiles):
            (complete if last else multiply)(q, t)
            if t >= 1:
                pair_sum(q, t - 1)
        pair_sum(q, tiles - 1)
        if q >= 1:
            finish(q - 1)
    for q in range(Q - 1):
        diagonal(q)
    finish(Q - 1)
    diagonal(Q - 1)
    for copy, condition in pending:
        if condition is None:
            copy.wait_send()
        else:
            pl.when(condition)(copy.wait_send)


def hand_over(cols_ref, diag_ref, cols_out, diag_out):
    cols_out[...] = cols_ref[...]
    diag_out[...] = diag_ref[...]


def body(R, C, inverse_block, factor_cols, diag_inverse, fill_mask):
    rows, cols = factor_cols.shape
    depth = inverse_block.shape[1]
    diag_rows, width = diag_inverse.shape[1:]
    X = max(n for n in range(1, R + 1) if R % n == 0 and n * n <= R)
    Z, G, M = R // X, R // C, C // 2
    halves = cols // LANES
    parts = split_rows(rows // 2, PARTS)
    blocks = rows // math.gcd(rows, width)
    tiles = max(n for n in range(1, TILES + 1) if blocks % n == 0)
    Q = 2 * halves
    J = Q * parts
    dma = pltpu.SemaphoreType.DMA
    vmem = pl.BlockSpec(memory_space=pltpu.VMEM)
    out_shape = (
        jax.ShapeDtypeStruct((rows, cols), jnp.bfloat16),
        jax.ShapeDtypeStruct(diag_inverse.shape, jnp.float32),
    )
    results = pl.pallas_call(
        functools.partial(kernel, R, C, X),
        out_shape=out_shape,
        in_specs=[pl.BlockSpec(memory_space=pltpu.SMEM), vmem, vmem, pl.BlockSpec(memory_space=pl.ANY)],
        out_specs=(vmem, vmem),
        scratch_shapes=[
            pltpu.VMEM(inverse_block.shape, jnp.bfloat16),
            pltpu.VMEM((halves, rows, LANES), jnp.bfloat16),
            pltpu.VMEM((Z, X, Q, rows // 2, LANES), jnp.bfloat16),
            pltpu.VMEM((Q, G, 2, rows // 2, M * LANES), jnp.bfloat16),
            pltpu.VMEM((Q, M, rows, LANES), jnp.float32),
            pltpu.VMEM((Q, M, rows, LANES), jnp.float32),
            pltpu.VMEM((halves, max(M - 1, 1), rows, LANES), jnp.float32),
            pltpu.VMEM((halves, max(M - 1, 1), rows, LANES), jnp.float32),
            pltpu.VMEM((halves, width, LANES), jnp.float32),
            pltpu.VMEM((halves, R - 1, diag_rows, LANES), jnp.float32),
            dma(()), dma((halves,)), dma((halves,)),
            dma((max(X - 1, 1), EARLY)), dma((X, EARLY)),
            dma((HOPS, 2, Z, X, J)), dma((Z, X, J)), dma((Z, X, J)), dma((G, C, J)),
            dma((max(X - 1, 1), G, J)), dma((G, J)),
            dma((Q, tiles)), dma((Q, tiles)),
            dma((Q, max(M - 1, 1), tiles)), dma((Q, max(M - 1, 1), tiles)),
            dma((halves, R - 1)), dma((halves, R - 1)),
        ],
        compiler_params=pltpu.CompilerParams(
            collective_id=0, has_side_effects=True, vmem_limit_bytes=60 << 20
        ),
        cost_estimate=pl.CostEstimate(
            flops=2 * rows * depth * cols * C, bytes_accessed=2 * rows * depth, transcendentals=0
        ),
    )(fill_mask.T, factor_cols, diag_inverse, inverse_block)
    return pl.pallas_call(
        hand_over,
        out_shape=out_shape,
        in_specs=[vmem, vmem],
        out_specs=(vmem, vmem),
    )(*results)


def solution(mesh):
    placed = (P("row", "col"), P("row", "col"), P("col", "row", None), P())
    return jax.shard_map(
        functools.partial(body, mesh.shape["row"], mesh.shape["col"]),
        mesh=mesh,
        in_specs=placed,
        out_specs=(P("row", "col"), P("col", "row", None)),
        check_vma=False,
    )
```

```python
import functools
import math

import jax
import jax.numpy as jnp
from jax import lax
from jax.experimental import pallas as pl
from jax.experimental.pallas import tpu as pltpu
from jax.sharding import PartitionSpec as P

LANES = 128
PARTS = 2
TILES = 5
DELAY = 1
HOPS = 1
AHEAD = 1
EARLY = 1
MESH = pl.DeviceIdType.MESH


def split_rows(extent, most):
    return max(n for n in range(1, most + 1) if extent % n == 0 and (extent // n) % 16 == 0)


def kernel(
    R, C, X, mask_ref, factor_ref, diag_ref, a_hbm, out_ref, diag_out_ref,
    a_ref, own_ref, zbuf, fbuf, part, pair_recv, ysend, yrecv, corr, corr_recv,
    a_sem, swap_send, swap_recv, e_send, e_recv, z_send, z_recv, b_send, f_recv, x_send, x_recv,
    p_send, p_recv, y_send, y_recv, c_send, c_recv,
):
    Z, G, M = R // X, R // C, C // 2
    rows, cols = factor_ref.shape
    halves = cols // LANES
    quarters = [(kk, half) for half in range(halves) for kk in range(2)]
    Q = len(quarters)
    width = diag_ref.shape[-1]
    diag_rows = diag_ref.shape[1]
    J, tiles = z_recv.shape[2], p_send.shape[1]
    parts = J // Q
    depth = rows // 2
    pr, mt = depth // parts, rows // tiles
    r, c = lax.axis_index("row"), lax.axis_index("col")
    z, x = r // X, r % X
    m, k = c // 2, c % 2
    partner = m * 2 + 1 - k
    pending = []

    a_copy = pltpu.make_async_copy(a_hbm, a_ref, a_sem)
    a_copy.start()

    barrier = pltpu.get_barrier_semaphore()
    for step in range(1, R):
        pl.semaphore_signal(barrier, inc=1, device_id=((r + step) % R, c), device_id_type=MESH)
    for step in range(1, C):
        pl.semaphore_signal(barrier, inc=1, device_id=(r, (c + step) % C), device_id_type=MESH)

    unit = math.gcd(rows, width)

    def mask_of(index, half):
        block = (r * rows + index * unit) // width
        node = c * (cols // width) + (half * LANES) // width
        return mask_ref[node, block].astype(jnp.float32)

    for half in range(halves):
        for index in range(rows // unit):
            there = pl.ds(index * unit, unit)
            value = factor_ref[there, half * LANES:(half + 1) * LANES].astype(jnp.float32)
            own_ref[half, there, :] = (value * mask_of(index, half)).astype(jnp.bfloat16)

    pl.semaphore_wait(barrier, R - 1 + C - 1)

    def start(copy, condition=None):
        pending.append((copy, condition))
        if condition is None:
            copy.start()
        else:
            pl.when(condition)(copy.start)

    def half_rows(index):
        return pl.ds(pl.multiple_of(index * depth, 16), depth)

    for half in range(halves):
        start(pltpu.make_async_remote_copy(
            src_ref=own_ref.at[half, half_rows(1 - k)], dst_ref=zbuf.at[z, x, half * 2 + k],
            send_sem=swap_send.at[half], recv_sem=swap_recv.at[half],
            device_id=(r, partner), device_id_type=MESH))
    for half in range(halves):
        zbuf[z, x, half * 2 + k] = own_ref[half, half_rows(k), :]

    def place(j):
        return j // parts, pl.ds((j % parts) * pr, pr)

    def early(j):
        return j >= J - EARLY

    def sources(j):
        return [x] + [(x + dx) % X for dx in range(1, X) if early(j)]

    def along_z(plane, xs, j, up, hops, condition):
        q, span = place(j)
        piece = zbuf.at[plane, xs, q, span]
        start(pltpu.make_async_remote_copy(
            src_ref=piece, dst_ref=piece,
            send_sem=z_send.at[hops - 1, 0 if up else 1, plane, xs, j], recv_sem=z_recv.at[plane, xs, j],
            device_id=(r + X * hops if up else r - X * hops, c), device_id_type=MESH), condition)

    def to_owner(plane, xs, j, condition):
        q, span = place(j)
        source = plane * X + xs
        owner, g = source // G, source % G
        dst = fbuf.at[q, g, k, span, pl.ds(pl.multiple_of(m * LANES, LANES), LANES)]
        piece = zbuf.at[plane, xs, q, span]
        here, away = owner == c, owner != c
        if condition is not None:
            here, away = jnp.logical_and(condition, here), jnp.logical_and(condition, away)
        local = pltpu.make_async_copy(piece, dst, f_recv.at[g, c, j])
        pl.when(here)(local.start)
        start(pltpu.make_async_remote_copy(
            src_ref=piece, dst_ref=dst, send_sem=b_send.at[plane, xs, j], recv_sem=f_recv.at[g, c, j],
            device_id=(r, owner), device_id_type=MESH), away)

    def swapped(q):
        kk, half = quarters[q]
        piece = zbuf.at[z, x, q]
        pl.when(k != kk)(pltpu.make_async_copy(piece, piece, swap_recv.at[half]).wait)

    def across(j):
        q, span = place(j)
        for dx in range(1, X):
            piece = zbuf.at[z, x, q, span]
            start(pltpu.make_async_remote_copy(
                src_ref=piece, dst_ref=piece,
                send_sem=e_send.at[dx - 1, j - (J - EARLY)], recv_sem=e_recv.at[x, j - (J - EARLY)],
                device_id=(z * X + (x + dx) % X, c), device_id_type=MESH))

    def own(j):
        q, span = place(j)
        if j % parts == 0 and q not in swaps:
            swapped(q)
            swaps.add(q)
        for xs in sources(j):
            if xs is not x:
                piece = zbuf.at[z, xs, q, span]
                pltpu.make_async_copy(piece, piece, e_recv.at[xs, j - (J - EARLY)]).wait()
            for hops in range(1, HOPS + 1):
                along_z(z, xs, j, True, hops, z + hops < Z)
                along_z(z, xs, j, False, hops, z >= hops)
            to_owner(z, xs, j, None)

    def arrivals(j, d):
        q, span = place(j)
        for xs in sources(j):
            for up in (True, False):
                plane = z - d if up else z + d
                there = z >= d if up else z + d < Z
                safe = jnp.clip(plane, 0, Z - 1)
                piece = zbuf.at[safe, xs, q, span]
                pl.when(there)(pltpu.make_async_copy(piece, piece, z_recv.at[safe, xs, j]).wait)
                if HOPS <= d < Z - 1:
                    onward = z + 1 < Z if up else z > 0
                    along_z(safe, xs, j, up, 1, jnp.logical_and(there, onward))
                to_owner(safe, xs, j, there)

    def collected(g, j):
        q, span = place(j)
        for other in range(C):
            piece = fbuf.at[q, g, other % 2, span, pl.ds(other // 2 * LANES, LANES)]
            pltpu.make_async_copy(piece, piece, f_recv.at[g, other, j]).wait()

    def forward(j):
        if early(j):
            return
        q, span = place(j)
        for g in range(G):
            mine = (G * c + g) % X == x
            whole = fbuf.at[q, g, :, span]

            pl.when(mine)(functools.partial(collected, g, j))
            for dx in range(1, X):
                start(pltpu.make_async_remote_copy(
                    src_ref=whole, dst_ref=whole, send_sem=x_send.at[dx - 1, g, j], recv_sem=x_recv.at[g, j],
                    device_id=(z * X + (x + dx) % X, c), device_id_type=MESH), mine)

    def gather_done(q, begun=False):
        if q == 0:
            a_copy.wait()
        for p in range(parts):
            j = q * parts + p
            _, span = place(j)
            for g in range(G):
                if early(j):
                    if begun:
                        pl.when(jnp.logical_not(mine(g)))(functools.partial(collected, g, j))
                    else:
                        collected(g, j)
                    continue
                whole = fbuf.at[q, g, :, span]
                pl.when((G * c + g) % X != x)(
                    pltpu.make_async_copy(whole, whole, x_recv.at[g, j]).wait)

    def mine(g):
        return (G * c + g) % X == x

    def add_group(q, g, t):
        span = pl.ds(t * mt, mt)
        panel = fbuf[q, g].reshape(rows, M * LANES)
        value = jnp.dot(a_ref[span, g * rows:(g + 1) * rows], panel, preferred_element_type=jnp.float32)
        for to in range(M):
            part[q, to, span, :] += value[:, to * LANES:(to + 1) * LANES]

    def begin(q):
        part[q] = jnp.zeros(part.shape[1:], jnp.float32)
        for g in range(G):
            @pl.when(mine(g))
            def _():
                for p in range(parts):
                    if early(q * parts + p):
                        collected(g, q * parts + p)
                for t in range(tiles):
                    add_group(q, g, t)

    def complete(q, t):
        for g in range(G):
            pl.when(jnp.logical_not(mine(g)))(functools.partial(add_group, q, g, t))
        send_pair(q, t)

    def send_pair(q, t):
        kk, _ = quarters[q]
        span = pl.ds(t * mt, mt)
        start(pltpu.make_async_remote_copy(
            src_ref=part.at[q, :, span], dst_ref=pair_recv.at[q, :, span],
            send_sem=p_send.at[q, t], recv_sem=p_recv.at[q, t],
            device_id=(r, partner), device_id_type=MESH), k != kk)

    def multiply(q, t):
        span = pl.ds(t * mt, mt)
        panel = fbuf[q].reshape(G * rows, M * LANES)
        value = jnp.dot(a_ref[span, :], panel, preferred_element_type=jnp.float32)
        for to in range(M):
            part[q, to, span, :] = value[:, to * LANES:(to + 1) * LANES]
        send_pair(q, t)

    def pair_sum(q, t):
        kk, half = quarters[q]
        span = pl.ds(t * mt, mt)
        piece = pair_recv.at[q, :, span]

        @pl.when(k == kk)
        def _():
            pltpu.make_async_copy(piece, piece, p_recv.at[q, t]).wait()
            for dm in range(1, M):
                to = (m + dm) % M
                ysend[half, dm - 1, span, :] = part[q, to, span, :] + pair_recv[q, to, span, :]

        for dm in range(1, M):
            to = (m + dm) % M
            start(pltpu.make_async_remote_copy(
                src_ref=ysend.at[half, dm - 1, span], dst_ref=yrecv.at[half, dm - 1, span],
                send_sem=y_send.at[q, dm - 1, t], recv_sem=y_recv.at[q, dm - 1, t],
                device_id=(r, to * 2 + k), device_id_type=MESH), k == kk)

    def finish(q):
        kk, half = quarters[q]
        lanes = slice(half * LANES, (half + 1) * LANES)

        @pl.when(k == kk)
        def _():
            for t in range(tiles):
                span = pl.ds(t * mt, mt)
                total = part[q, m, span, :] + pair_recv[q, m, span, :]
                for dm in range(1, M):
                    piece = yrecv.at[half, dm - 1, span]
                    pltpu.make_async_copy(piece, piece, y_recv.at[q, dm - 1, t]).wait()
                    total = total + yrecv[half, dm - 1, span, :]
                for index in range(mt // unit):
                    value = -total[index * unit:(index + 1) * unit] * mask_of(t * (mt // unit) + index, half)
                    out_ref[pl.ds(t * mt + index * unit, unit), lanes] = value.astype(jnp.bfloat16)
                for left in range(halves):
                    there = slice(left * LANES, (left + 1) * LANES)
                    product = lax.dot_general(
                        own_ref[left, span, :], out_ref[span, lanes], (((0,), (0,)), ((), ())),
                        preferred_element_type=jnp.float32)
                    if t == 0:
                        corr[half, there, :] = product
                    else:
                        corr[half, there, :] += product

        for step in range(1, R):
            to = (r + step) % R
            start(pltpu.make_async_remote_copy(
                src_ref=corr.at[half, pl.ds(pl.multiple_of(to * diag_rows, 8), diag_rows)],
                dst_ref=corr_recv.at[half, step - 1],
                send_sem=c_send.at[half, step - 1], recv_sem=c_recv.at[half, step - 1],
                device_id=(to, c), device_id_type=MESH), k == kk)

    def diagonal(q):
        kk, half = quarters[q]
        lanes = slice(half * LANES, (half + 1) * LANES)

        @pl.when(k == kk)
        def _():
            total = corr[half, pl.ds(pl.multiple_of(r * diag_rows, 8), diag_rows), :]
            for step in range(1, R):
                piece = corr_recv.at[half, step - 1]
                pltpu.make_async_copy(piece, piece, c_recv.at[half, step - 1]).wait()
                total = total + corr_recv[half, step - 1]
            diag_out_ref[0, :, lanes] = diag_ref[0, :, lanes] - total

    def work(q):
        def first():
            gather_done(q)
            multiply(q, 0)

        def sums():
            for t in range(tiles):
                pair_sum(q, t)

        jobs = [first] + [functools.partial(multiply, q, t) for t in range(1, tiles)] + [sums]
        if q >= 1:
            jobs.append(functools.partial(finish, q - 1))
        return jobs

    swaps = set()
    for j in range(min(AHEAD, J)):
        own(j)
    for j in range(J - EARLY, J):
        if j // parts not in swaps:
            swapped(j // parts)
            swaps.add(j // parts)
        across(j)
    jobs, done, sent = [], 0, 0
    for s in range(J + max(Z - 2, 0)):
        for d in range(1, Z):
            if 0 <= s - d + 1 < J:
                arrivals(s - d + 1, d)
            if d == 1 and s + AHEAD < J:
                own(s + AHEAD)
            if d == max(Z - 2, 1) and s >= Z - 1:
                forward(s - Z + 1)
                sent = s - Z + 2
            if jobs:
                jobs.pop(0)()
        if sent - DELAY >= (done + 1) * parts:
            jobs += work(done)
            done += 1
    for j in range(sent, J):
        forward(j)
    for job in jobs:
        job()
    for q in range(done, Q):
        last = q == Q - 1 and q > 0
        if last:
            begin(q)
        gather_done(q, last)
        for t in range(tiles):
            (complete if last else multiply)(q, t)
            if t >= 1:
                pair_sum(q, t - 1)
        pair_sum(q, tiles - 1)
        if q >= 1:
            finish(q - 1)
    for q in range(Q - 1):
        diagonal(q)
    finish(Q - 1)
    diagonal(Q - 1)
    for copy, condition in pending:
        if condition is None:
            copy.wait_send()
        else:
            pl.when(condition)(copy.wait_send)


def hand_over(cols_ref, diag_ref, cols_out, diag_out):
    cols_out[...] = cols_ref[...]
    diag_out[...] = diag_ref[...]


def body(R, C, inverse_block, factor_cols, diag_inverse, fill_mask):
    rows, cols = factor_cols.shape
    depth = inverse_block.shape[1]
    diag_rows, width = diag_inverse.shape[1:]
    X = max(n for n in range(1, R + 1) if R % n == 0 and n * n <= R)
    Z, G, M = R // X, R // C, C // 2
    halves = cols // LANES
    parts = split_rows(rows // 2, PARTS)
    blocks = rows // math.gcd(rows, width)
    tiles = max(n for n in range(1, TILES + 1) if blocks % n == 0)
    Q = 2 * halves
    J = Q * parts
    dma = pltpu.SemaphoreType.DMA
    vmem = pl.BlockSpec(memory_space=pltpu.VMEM)
    out_shape = (
        jax.ShapeDtypeStruct((rows, cols), jnp.bfloat16),
        jax.ShapeDtypeStruct(diag_inverse.shape, jnp.float32),
    )
    results = pl.pallas_call(
        functools.partial(kernel, R, C, X),
        out_shape=out_shape,
        in_specs=[pl.BlockSpec(memory_space=pltpu.SMEM), vmem, vmem, pl.BlockSpec(memory_space=pl.ANY)],
        out_specs=(vmem, vmem),
        scratch_shapes=[
            pltpu.VMEM(inverse_block.shape, jnp.bfloat16),
            pltpu.VMEM((halves, rows, LANES), jnp.bfloat16),
            pltpu.VMEM((Z, X, Q, rows // 2, LANES), jnp.bfloat16),
            pltpu.VMEM((Q, G, 2, rows // 2, M * LANES), jnp.bfloat16),
            pltpu.VMEM((Q, M, rows, LANES), jnp.float32),
            pltpu.VMEM((Q, M, rows, LANES), jnp.float32),
            pltpu.VMEM((halves, max(M - 1, 1), rows, LANES), jnp.float32),
            pltpu.VMEM((halves, max(M - 1, 1), rows, LANES), jnp.float32),
            pltpu.VMEM((halves, width, LANES), jnp.float32),
            pltpu.VMEM((halves, R - 1, diag_rows, LANES), jnp.float32),
            dma(()), dma((halves,)), dma((halves,)),
            dma((max(X - 1, 1), EARLY)), dma((X, EARLY)),
            dma((HOPS, 2, Z, X, J)), dma((Z, X, J)), dma((Z, X, J)), dma((G, C, J)),
            dma((max(X - 1, 1), G, J)), dma((G, J)),
            dma((Q, tiles)), dma((Q, tiles)),
            dma((Q, max(M - 1, 1), tiles)), dma((Q, max(M - 1, 1), tiles)),
            dma((halves, R - 1)), dma((halves, R - 1)),
        ],
        compiler_params=pltpu.CompilerParams(
            collective_id=0, has_side_effects=True, vmem_limit_bytes=60 << 20
        ),
        cost_estimate=pl.CostEstimate(
            flops=2 * rows * depth * cols * C, bytes_accessed=2 * rows * depth, transcendentals=0
        ),
    )(fill_mask.T, factor_cols, diag_inverse, inverse_block)
    return pl.pallas_call(
        hand_over,
        out_shape=out_shape,
        in_specs=[vmem, vmem],
        out_specs=(vmem, vmem),
    )(*results)


def solution(mesh):
    placed = (P("row", "col"), P("row", "col"), P("col", "row", None), P())
    return jax.shard_map(
        functools.partial(body, mesh.shape["row"], mesh.shape["col"]),
        mesh=mesh,
        in_specs=placed,
        out_specs=(P("row", "col"), P("col", "row", None)),
        check_vma=False,
    )
```

```python
import functools
import math

import jax
import jax.numpy as jnp
from jax import lax
from jax.experimental import pallas as pl
from jax.experimental.pallas import tpu as pltpu
from jax.sharding import PartitionSpec as P

LANES = 128
PARTS = 2
TILES = 5
DELAY = 1
HOPS = 1
AHEAD = 1
EARLY = 2
MESH = pl.DeviceIdType.MESH


def split_rows(extent, most):
    return max(n for n in range(1, most + 1) if extent % n == 0 and (extent // n) % 16 == 0)


def kernel(
    R, C, X, mask_ref, factor_ref, diag_ref, a_hbm, out_ref, diag_out_ref,
    a_ref, own_ref, zbuf, fbuf, part, pair_recv, ysend, yrecv, corr, corr_recv,
    a_sem, swap_send, swap_recv, e_send, e_recv, z_send, z_recv, b_send, f_recv, x_send, x_recv,
    p_send, p_recv, y_send, y_recv, c_send, c_recv,
):
    Z, G, M = R // X, R // C, C // 2
    rows, cols = factor_ref.shape
    halves = cols // LANES
    quarters = [(kk, half) for half in range(halves) for kk in range(2)]
    Q = len(quarters)
    width = diag_ref.shape[-1]
    diag_rows = diag_ref.shape[1]
    J, tiles = z_recv.shape[2], p_send.shape[1]
    parts = J // Q
    depth = rows // 2
    pr, mt = depth // parts, rows // tiles
    r, c = lax.axis_index("row"), lax.axis_index("col")
    z, x = r // X, r % X
    m, k = c // 2, c % 2
    partner = m * 2 + 1 - k
    pending = []

    a_copy = pltpu.make_async_copy(a_hbm, a_ref, a_sem)
    a_copy.start()

    barrier = pltpu.get_barrier_semaphore()
    for step in range(1, R):
        pl.semaphore_signal(barrier, inc=1, device_id=((r + step) % R, c), device_id_type=MESH)
    for step in range(1, C):
        pl.semaphore_signal(barrier, inc=1, device_id=(r, (c + step) % C), device_id_type=MESH)

    unit = math.gcd(rows, width)

    def mask_of(index, half):
        block = (r * rows + index * unit) // width
        node = c * (cols // width) + (half * LANES) // width
        return mask_ref[node, block].astype(jnp.float32)

    for half in range(halves):
        for index in range(rows // unit):
            there = pl.ds(index * unit, unit)
            value = factor_ref[there, half * LANES:(half + 1) * LANES].astype(jnp.float32)
            own_ref[half, there, :] = (value * mask_of(index, half)).astype(jnp.bfloat16)

    pl.semaphore_wait(barrier, R - 1 + C - 1)

    def start(copy, condition=None):
        pending.append((copy, condition))
        if condition is None:
            copy.start()
        else:
            pl.when(condition)(copy.start)

    def half_rows(index):
        return pl.ds(pl.multiple_of(index * depth, 16), depth)

    for half in range(halves):
        start(pltpu.make_async_remote_copy(
            src_ref=own_ref.at[half, half_rows(1 - k)], dst_ref=zbuf.at[z, x, half * 2 + k],
            send_sem=swap_send.at[half], recv_sem=swap_recv.at[half],
            device_id=(r, partner), device_id_type=MESH))
    for half in range(halves):
        zbuf[z, x, half * 2 + k] = own_ref[half, half_rows(k), :]

    def place(j):
        return j // parts, pl.ds((j % parts) * pr, pr)

    def early(j):
        return j >= J - EARLY

    def sources(j):
        return [x] + [(x + dx) % X for dx in range(1, X) if early(j)]

    def along_z(plane, xs, j, up, hops, condition):
        q, span = place(j)
        piece = zbuf.at[plane, xs, q, span]
        start(pltpu.make_async_remote_copy(
            src_ref=piece, dst_ref=piece,
            send_sem=z_send.at[hops - 1, 0 if up else 1, plane, xs, j], recv_sem=z_recv.at[plane, xs, j],
            device_id=(r + X * hops if up else r - X * hops, c), device_id_type=MESH), condition)

    def to_owner(plane, xs, j, condition):
        q, span = place(j)
        source = plane * X + xs
        owner, g = source // G, source % G
        dst = fbuf.at[q, g, k, span, pl.ds(pl.multiple_of(m * LANES, LANES), LANES)]
        piece = zbuf.at[plane, xs, q, span]
        here, away = owner == c, owner != c
        if condition is not None:
            here, away = jnp.logical_and(condition, here), jnp.logical_and(condition, away)
        local = pltpu.make_async_copy(piece, dst, f_recv.at[g, c, j])
        pl.when(here)(local.start)
        start(pltpu.make_async_remote_copy(
            src_ref=piece, dst_ref=dst, send_sem=b_send.at[plane, xs, j], recv_sem=f_recv.at[g, c, j],
            device_id=(r, owner), device_id_type=MESH), away)

    def swapped(q):
        kk, half = quarters[q]
        piece = zbuf.at[z, x, q]
        pl.when(k != kk)(pltpu.make_async_copy(piece, piece, swap_recv.at[half]).wait)

    def across(j):
        q, span = place(j)
        for dx in range(1, X):
            piece = zbuf.at[z, x, q, span]
            start(pltpu.make_async_remote_copy(
                src_ref=piece, dst_ref=piece,
                send_sem=e_send.at[dx - 1, j - (J - EARLY)], recv_sem=e_recv.at[x, j - (J - EARLY)],
                device_id=(z * X + (x + dx) % X, c), device_id_type=MESH))

    def own(j):
        q, span = place(j)
        if j % parts == 0 and q not in swaps:
            swapped(q)
            swaps.add(q)
        for xs in sources(j):
            if xs is not x:
                piece = zbuf.at[z, xs, q, span]
                pltpu.make_async_copy(piece, piece, e_recv.at[xs, j - (J - EARLY)]).wait()
            for hops in range(1, HOPS + 1):
                along_z(z, xs, j, True, hops, z + hops < Z)
                along_z(z, xs, j, False, hops, z >= hops)
            to_owner(z, xs, j, None)

    def arrivals(j, d):
        q, span = place(j)
        for xs in sources(j):
            for up in (True, False):
                plane = z - d if up else z + d
                there = z >= d if up else z + d < Z
                safe = jnp.clip(plane, 0, Z - 1)
                piece = zbuf.at[safe, xs, q, span]
                pl.when(there)(pltpu.make_async_copy(piece, piece, z_recv.at[safe, xs, j]).wait)
                if HOPS <= d < Z - 1:
                    onward = z + 1 < Z if up else z > 0
                    along_z(safe, xs, j, up, 1, jnp.logical_and(there, onward))
                to_owner(safe, xs, j, there)

    def collected(g, j):
        q, span = place(j)
        for other in range(C):
            piece = fbuf.at[q, g, other % 2, span, pl.ds(other // 2 * LANES, LANES)]
            pltpu.make_async_copy(piece, piece, f_recv.at[g, other, j]).wait()

    def forward(j):
        if early(j):
            return
        q, span = place(j)
        for g in range(G):
            mine = (G * c + g) % X == x
            whole = fbuf.at[q, g, :, span]

            pl.when(mine)(functools.partial(collected, g, j))
            for dx in range(1, X):
                start(pltpu.make_async_remote_copy(
                    src_ref=whole, dst_ref=whole, send_sem=x_send.at[dx - 1, g, j], recv_sem=x_recv.at[g, j],
                    device_id=(z * X + (x + dx) % X, c), device_id_type=MESH), mine)

    def gather_done(q, begun=False):
        if q == 0:
            a_copy.wait()
        for p in range(parts):
            j = q * parts + p
            _, span = place(j)
            for g in range(G):
                if early(j):
                    if begun:
                        pl.when(jnp.logical_not(mine(g)))(functools.partial(collected, g, j))
                    else:
                        collected(g, j)
                    continue
                whole = fbuf.at[q, g, :, span]
                pl.when((G * c + g) % X != x)(
                    pltpu.make_async_copy(whole, whole, x_recv.at[g, j]).wait)

    def mine(g):
        return (G * c + g) % X == x

    def add_group(q, g, t):
        span = pl.ds(t * mt, mt)
        panel = fbuf[q, g].reshape(rows, M * LANES)
        value = jnp.dot(a_ref[span, g * rows:(g + 1) * rows], panel, preferred_element_type=jnp.float32)
        for to in range(M):
            part[q, to, span, :] += value[:, to * LANES:(to + 1) * LANES]

    def begin(q):
        part[q] = jnp.zeros(part.shape[1:], jnp.float32)
        for g in range(G):
            @pl.when(mine(g))
            def _():
                for p in range(parts):
                    if early(q * parts + p):
                        collected(g, q * parts + p)
                for t in range(tiles):
                    add_group(q, g, t)

    def complete(q, t):
        for g in range(G):
            pl.when(jnp.logical_not(mine(g)))(functools.partial(add_group, q, g, t))
        send_pair(q, t)

    def send_pair(q, t):
        kk, _ = quarters[q]
        span = pl.ds(t * mt, mt)
        start(pltpu.make_async_remote_copy(
            src_ref=part.at[q, :, span], dst_ref=pair_recv.at[q, :, span],
            send_sem=p_send.at[q, t], recv_sem=p_recv.at[q, t],
            device_id=(r, partner), device_id_type=MESH), k != kk)

    def multiply(q, t):
        span = pl.ds(t * mt, mt)
        panel = fbuf[q].reshape(G * rows, M * LANES)
        value = jnp.dot(a_ref[span, :], panel, preferred_element_type=jnp.float32)
        for to in range(M):
            part[q, to, span, :] = value[:, to * LANES:(to + 1) * LANES]
        send_pair(q, t)

    def pair_sum(q, t):
        kk, half = quarters[q]
        span = pl.ds(t * mt, mt)
        piece = pair_recv.at[q, :, span]

        @pl.when(k == kk)
        def _():
            pltpu.make_async_copy(piece, piece, p_recv.at[q, t]).wait()
            for dm in range(1, M):
                to = (m + dm) % M
                ysend[half, dm - 1, span, :] = part[q, to, span, :] + pair_recv[q, to, span, :]

        for dm in range(1, M):
            to = (m + dm) % M
            start(pltpu.make_async_remote_copy(
                src_ref=ysend.at[half, dm - 1, span], dst_ref=yrecv.at[half, dm - 1, span],
                send_sem=y_send.at[q, dm - 1, t], recv_sem=y_recv.at[q, dm - 1, t],
                device_id=(r, to * 2 + k), device_id_type=MESH), k == kk)

    def finish(q):
        kk, half = quarters[q]
        lanes = slice(half * LANES, (half + 1) * LANES)

        @pl.when(k == kk)
        def _():
            for t in range(tiles):
                span = pl.ds(t * mt, mt)
                total = part[q, m, span, :] + pair_recv[q, m, span, :]
                for dm in range(1, M):
                    piece = yrecv.at[half, dm - 1, span]
                    pltpu.make_async_copy(piece, piece, y_recv.at[q, dm - 1, t]).wait()
                    total = total + yrecv[half, dm - 1, span, :]
                for index in range(mt // unit):
                    value = -total[index * unit:(index + 1) * unit] * mask_of(t * (mt // unit) + index, half)
                    out_ref[pl.ds(t * mt + index * unit, unit), lanes] = value.astype(jnp.bfloat16)
                for left in range(halves):
                    there = slice(left * LANES, (left + 1) * LANES)
                    product = lax.dot_general(
                        own_ref[left, span, :], out_ref[span, lanes], (((0,), (0,)), ((), ())),
                        preferred_element_type=jnp.float32)
                    if t == 0:
                        corr[half, there, :] = product
                    else:
                        corr[half, there, :] += product

        for step in range(1, R):
            to = (r + step) % R
            start(pltpu.make_async_remote_copy(
                src_ref=corr.at[half, pl.ds(pl.multiple_of(to * diag_rows, 8), diag_rows)],
                dst_ref=corr_recv.at[half, step - 1],
                send_sem=c_send.at[half, step - 1], recv_sem=c_recv.at[half, step - 1],
                device_id=(to, c), device_id_type=MESH), k == kk)

    def diagonal(q):
        kk, half = quarters[q]
        lanes = slice(half * LANES, (half + 1) * LANES)

        @pl.when(k == kk)
        def _():
            total = corr[half, pl.ds(pl.multiple_of(r * diag_rows, 8), diag_rows), :]
            for step in range(1, R):
                piece = corr_recv.at[half, step - 1]
                pltpu.make_async_copy(piece, piece, c_recv.at[half, step - 1]).wait()
                total = total + corr_recv[half, step - 1]
            diag_out_ref[0, :, lanes] = diag_ref[0, :, lanes] - total

    def work(q):
        def first():
            gather_done(q)
            multiply(q, 0)

        def sums():
            for t in range(tiles):
                pair_sum(q, t)

        jobs = [first] + [functools.partial(multiply, q, t) for t in range(1, tiles)] + [sums]
        if q >= 1:
            jobs.append(functools.partial(finish, q - 1))
        return jobs

    swaps = set()
    for j in range(min(AHEAD, J)):
        own(j)
    for j in range(J - EARLY, J):
        if j // parts not in swaps:
            swapped(j // parts)
            swaps.add(j // parts)
        across(j)
    jobs, done = [], 0
    for j in range(J):
        for d in range(1, Z):
            arrivals(j, d)
            if d == 1 and j + AHEAD < J:
                own(j + AHEAD)
            if d == max(Z - 2, 1) and j >= 1:
                forward(j - 1)
            if jobs:
                jobs.pop(0)()
        if j - DELAY >= (done + 1) * parts:
            jobs += work(done)
            done += 1
    forward(J - 1)
    for job in jobs:
        job()
    for q in range(done, Q):
        last = q == Q - 1 and q > 0
        if last:
            begin(q)
        gather_done(q, last)
        for t in range(tiles):
            (complete if last else multiply)(q, t)
            if t >= 1:
                pair_sum(q, t - 1)
        pair_sum(q, tiles - 1)
        if q >= 1:
            finish(q - 1)
    for q in range(Q - 1):
        diagonal(q)
    finish(Q - 1)
    diagonal(Q - 1)
    for copy, condition in pending:
        if condition is None:
            copy.wait_send()
        else:
            pl.when(condition)(copy.wait_send)


def hand_over(cols_ref, diag_ref, cols_out, diag_out):
    cols_out[...] = cols_ref[...]
    diag_out[...] = diag_ref[...]


def body(R, C, inverse_block, factor_cols, diag_inverse, fill_mask):
    rows, cols = factor_cols.shape
    depth = inverse_block.shape[1]
    diag_rows, width = diag_inverse.shape[1:]
    X = max(n for n in range(1, R + 1) if R % n == 0 and n * n <= R)
    Z, G, M = R // X, R // C, C // 2
    halves = cols // LANES
    parts = split_rows(rows // 2, PARTS)
    blocks = rows // math.gcd(rows, width)
    tiles = max(n for n in range(1, TILES + 1) if blocks % n == 0)
    Q = 2 * halves
    J = Q * parts
    dma = pltpu.SemaphoreType.DMA
    vmem = pl.BlockSpec(memory_space=pltpu.VMEM)
    out_shape = (
        jax.ShapeDtypeStruct((rows, cols), jnp.bfloat16),
        jax.ShapeDtypeStruct(diag_inverse.shape, jnp.float32),
    )
    results = pl.pallas_call(
        functools.partial(kernel, R, C, X),
        out_shape=out_shape,
        in_specs=[pl.BlockSpec(memory_space=pltpu.SMEM), vmem, vmem, pl.BlockSpec(memory_space=pl.ANY)],
        out_specs=(vmem, vmem),
        scratch_shapes=[
            pltpu.VMEM(inverse_block.shape, jnp.bfloat16),
            pltpu.VMEM((halves, rows, LANES), jnp.bfloat16),
            pltpu.VMEM((Z, X, Q, rows // 2, LANES), jnp.bfloat16),
            pltpu.VMEM((Q, G, 2, rows // 2, M * LANES), jnp.bfloat16),
            pltpu.VMEM((Q, M, rows, LANES), jnp.float32),
            pltpu.VMEM((Q, M, rows, LANES), jnp.float32),
            pltpu.VMEM((halves, max(M - 1, 1), rows, LANES), jnp.float32),
            pltpu.VMEM((halves, max(M - 1, 1), rows, LANES), jnp.float32),
            pltpu.VMEM((halves, width, LANES), jnp.float32),
            pltpu.VMEM((halves, R - 1, diag_rows, LANES), jnp.float32),
            dma(()), dma((halves,)), dma((halves,)),
            dma((max(X - 1, 1), EARLY)), dma((X, EARLY)),
            dma((HOPS, 2, Z, X, J)), dma((Z, X, J)), dma((Z, X, J)), dma((G, C, J)),
            dma((max(X - 1, 1), G, J)), dma((G, J)),
            dma((Q, tiles)), dma((Q, tiles)),
            dma((Q, max(M - 1, 1), tiles)), dma((Q, max(M - 1, 1), tiles)),
            dma((halves, R - 1)), dma((halves, R - 1)),
        ],
        compiler_params=pltpu.CompilerParams(
            collective_id=0, has_side_effects=True, vmem_limit_bytes=60 << 20
        ),
        cost_estimate=pl.CostEstimate(
            flops=2 * rows * depth * cols * C, bytes_accessed=2 * rows * depth, transcendentals=0
        ),
    )(fill_mask.T, factor_cols, diag_inverse, inverse_block)
    return pl.pallas_call(
        hand_over,
        out_shape=out_shape,
        in_specs=[vmem, vmem],
        out_specs=(vmem, vmem),
    )(*results)


def solution(mesh):
    placed = (P("row", "col"), P("row", "col"), P("col", "row", None), P())
    return jax.shard_map(
        functools.partial(body, mesh.shape["row"], mesh.shape["col"]),
        mesh=mesh,
        in_specs=placed,
        out_specs=(P("row", "col"), P("col", "row", None)),
        check_vma=False,
    )
```
